1024 devices in a mesh: by: 64 (over z, core), bx: 16 (over y, x).
Axes of the slice: x: 4, y: 4, z: 32, core: 2. Of those that a mesh axis runs over, the one named last changes fastest.
Arguments:
- temp: float32 [48, 512, 2048], P(None, 'by', 'bx'), may hold values from -6 to 6
- uvel: float32 [48, 512, 2048], P(None, 'by', 'bx'), may hold values from -6 to 6
- vvel: float32 [48, 512, 2048], P(None, 'by', 'bx'), may hold values from -6 to 6
- kmt: int32 [512, 2048], P('by', 'bx'), may hold values from 0 to 48, as said below
Outputs:
- temp_new: float32 [48, 512, 2048], P(None, 'by', 'bx')
- uvel_new: float32 [48, 512, 2048], P(None, 'by', 'bx')
- vvel_new: float32 [48, 512, 2048], P(None, 'by', 'bx')
- surface: float32 [512, 2048], P('by', 'bx')
- residual: float32 [512, 2048], P('by', 'bx')
The draws below stay inside these ranges and needn't reach their ends.
Inputs may be any that keep to these rules, and one draw needn't show every extreme that they name: kmt is 0 on land; land comes in patches of 4 x 4 cells; ocean columns have 1 to 48 active levels.
All inputs are finite; a program needn't handle non-finite values.
Results may differ from the reference program's by a relative error of at most 0.0012.
Values sent between devices are 32-bit elements; how exact they have to be, the bound alone decides.
A program may use at most 32 MiB of HBM per device.

```python
import math
import jax
import jax.numpy as jnp
from jax import lax

KL = 48
ITERS = 3
NY = 512
NX = 2048


def draw_kmt(key, part):
    key = jax.random.fold_in(key, 7)
    patch_key, depth_key = jax.random.split(key)
    coarse = jax.random.randint(patch_key, (NY // 4, NX // 4), 0, 4)
    land = jnp.repeat(jnp.repeat(coarse == 0, 4, axis=0), 4, axis=1)
    depth = jax.random.randint(depth_key, (NY, NX), 1, KL + 1)
    return jnp.where(land, 0, depth).astype(jnp.int32)


def block_scale(rng, shape, cuts, least, high):
    factor_of = 1.0
    for axis_at, shards_of in cuts:
        draws = jax.random.uniform(jax.random.fold_in(jax.random.fold_in(rng, 6), axis_at), (shards_of,), jnp.float32, least / len(cuts), high / len(cuts))
        factor_of = factor_of * jnp.repeat(jnp.exp(draws), shape[axis_at] // shards_of).reshape((-1,) + (1,) * (len(shape) - 1 - axis_at))
    return factor_of


def gaussian(own_key, shape, scale, bound, cuts=(), held_as=jnp.bfloat16):
    entries = scale * jax.random.normal(own_key, shape, jnp.float32)
    if cuts:
        entries = entries * block_scale(own_key, shape, cuts, -0.22, 0.18)
    return jnp.clip(entries, -bound, bound).astype(held_as)


def setup_inputs(seed: int = 0) -> dict:
    key_of = jax.random.split(jax.random.key(seed), 5)
    temp = gaussian(key_of[0], (KL, NY, NX), 1.0, 6.0, ((1, 64), (2, 16)), jnp.float32)
    uvel = gaussian(key_of[1], (KL, NY, NX), 1.0, 6.0, ((1, 64), (2, 16)), jnp.float32)
    vvel = gaussian(key_of[2], (KL, NY, NX), 1.0, 6.0, ((1, 64), (2, 16)), jnp.float32)
    kmt = draw_kmt(jax.random.fold_in(key_of[4], 71), 0)
    return dict(temp=temp, uvel=uvel, vvel=vvel, kmt=kmt)


STEP_DIFF = 0.1
STEP_ADV = 0.5
STEP_SMOOTH = 0.1
STEP_VERT = 0.2
SURFACE_TERM = 0.25

def faces(padded):
    return (padded[..., 1:-1, 2:], padded[..., 1:-1, :-2], padded[..., 2:, 1:-1], padded[..., :-2, 1:-1])

def centre(padded):
    return padded[..., 1:-1, 1:-1]

def level_mask(depth, levels):
    index = lax.broadcasted_iota(jnp.int32, (levels,) + depth.shape, 0).astype(jnp.float32)
    return (index < depth[None]).astype(jnp.float32)

def laplace(field_p, mask_p):
    field_c = centre(field_p)
    mask_c = centre(mask_p)
    total = jnp.zeros_like(field_c)
    for field_n, mask_n in zip(faces(field_p), faces(mask_p)):
        total = total + mask_c * mask_n * (field_n - field_c)
    return total

def section_one(field_p, mask_p):
    field_c = centre(field_p)
    east, west, north, south = faces(field_p)
    advect = 0.5 * (field_c[1] * (east - west) + field_c[2] * (north - south))
    return centre(mask_p) * (field_c + STEP_DIFF * laplace(field_p, mask_p) - STEP_ADV * advect)

def vertical(field, mask):
    zero_f = jnp.zeros_like(field[:, :1])
    zero_m = jnp.zeros_like(mask[:1])
    field_up = jnp.concatenate([field[:, 1:], zero_f], axis=1)
    field_dn = jnp.concatenate([zero_f, field[:, :-1]], axis=1)
    mask_up = jnp.concatenate([mask[1:], zero_m], axis=0)
    mask_dn = jnp.concatenate([zero_m, mask[:-1]], axis=0)
    return mask * (mask_up * (field_up - field) + mask_dn * (field_dn - field))

def section_two(star_p, mask_p):
    star_c = centre(star_p)
    mask_c = centre(mask_p)
    return mask_c * (star_c + STEP_SMOOTH * laplace(star_p, mask_p) + STEP_VERT * vertical(star_c, mask_c))

def face_weights(depth_p, levels):
    height = depth_p / float(levels)
    height_c = centre(height)
    weights = [jnp.minimum(height_c, height_n) for height_n in faces(height)]
    diag = SURFACE_TERM + weights[0] + weights[1] + weights[2] + weights[3]
    return (weights, diag)

def apply_surface(field_p, weights, diag):
    result = diag * centre(field_p)
    for weight, field_n in zip(weights, faces(field_p)):
        result = result - weight * field_n
    return result

def pad_grid(array, width):
    ndim = array.ndim
    wrapped = jnp.pad(array, [(0, 0)] * (ndim - 1) + [(width, width)], mode='wrap')
    return jnp.pad(wrapped, [(0, 0)] * (ndim - 2) + [(width, width), (0, 0)])

def reference(temp, uvel, vvel, kmt):
    levels = temp.shape[0]
    depth = kmt.astype(jnp.float32)
    fields = jnp.stack([temp, uvel, vvel])
    mask = level_mask(depth, levels)
    field_p = pad_grid(fields, 2)
    mask_p = pad_grid(mask, 2)
    star = section_one(field_p, mask_p)
    updated = section_two(star, centre(mask_p))
    rhs = lax.optimization_barrier(jnp.sum(updated[0], axis=0)) / math.sqrt(levels)
    weights, diag = face_weights(pad_grid(depth, 1), levels)
    inverse = 1.0 / diag
    solution = jnp.zeros_like(rhs)
    resid = rhs
    precond = resid * inverse
    direction = precond
    rz_now = jnp.sum(resid * precond)
    for step in range(ITERS):
        image = apply_surface(pad_grid(direction, 1), weights, diag)
        alpha = rz_now / jnp.sum(direction * image)
        solution = solution + alpha * direction
        resid = resid - alpha * image
        if step + 1 < ITERS:
            precond = resid * inverse
            rz_next = jnp.sum(resid * precond)
            direction = precond + rz_next / rz_now * direction
            rz_now = rz_next
    return (updated[0], updated[1], updated[2], solution, resid)
```

```python
import math

import jax
import jax.numpy as jnp
from jax import lax
from jax.experimental import pallas as pl
from jax.experimental.pallas import tpu as pltpu
from jax.sharding import PartitionSpec as P

ITERS = 3
STEP_DIFF = 0.1
STEP_ADV = 0.5
STEP_SMOOTH = 0.1
STEP_VERT = 0.2
SURFACE_TERM = 0.25

KL, ROWS, COLS = 48, 8, 128
CHUNK = 8
PITCH = 16
PADDED = PITCH * (KL + 2)
RADIUS = 4

F32 = jnp.float32
MESH = pl.DeviceIdType.MESH

DIRS = [(-1, -1), (-1, 0), (-1, 1), (0, -1), (0, 1), (1, -1), (1, 0), (1, 1)]
SW, S, SE, W, E, NW, N, NE = range(8)

GRAM = [(i, j) for i in range(ITERS + 1) for j in range(i, ITERS + 1)]


def roll(value, shift, axis):
    size = value.shape[axis]
    return pltpu.roll(value, shift % size if isinstance(shift, int) else shift, axis)


def lanes_of(shape):
    return lax.broadcasted_iota(jnp.int32, shape, len(shape) - 1)


def east_west(value, edge):
    lane = lanes_of(value.shape)
    axis = value.ndim - 1
    east = roll(jnp.where(lane == 0, edge, value), -1, axis)
    west = roll(jnp.where(lane == COLS - 1, edge, value), 1, axis)
    return east, west


def star_terms(level, depths, uvel, vvel):
    centre = level < depths[0]
    diff = [jnp.where(level < d, F32(STEP_DIFF), F32(0.0)) for d in depths[1:]]
    own = F32(1.0) - ((diff[0] + diff[1]) + (diff[2] + diff[3]))
    adv_u = F32(0.5 * STEP_ADV) * uvel
    adv_v = F32(0.5 * STEP_ADV) * vvel
    return centre, own, (diff[0] - adv_u, diff[1] + adv_u, diff[2] - adv_v, diff[3] + adv_v)


def star_value(terms, cell, sides):
    centre, own, factors = terms
    total = own * cell
    for factor, side in zip(factors, sides):
        total = total + factor * side
    return jnp.where(centre, total, F32(0.0))


def kernel(
    nby, nbx,
    temp_in, uvel_in, vvel_in, kmt_in,
    temp_out, uvel_out, vvel_out, surface_out, resid_out,
    raw, kmt_v, pad_t, pad_u, pad_v, star_t, star_u, star_v, fresh, surf_v, resid_v, depth_v, depths_v, q_ref, qs_ref,
    tx_row1, tx_row2, tx_col, tx_cor, rx_row1, rx_row2, rx_col, rx_cor,
    tx_u, rx_u, tx_bx, rx_bx, tx_by, rx_by,
    in_sem, out_sem, row1_s, row1_r, row2_s, row2_r, col_s, col_r, cor_s, cor_r, u_s, u_r, bx_s, bx_r, by_s, by_r,
    known,
):
    by, bx = lax.axis_index("by"), lax.axis_index("bx")
    pads = (pad_t, pad_u, pad_v)
    stars = (star_t, star_u, star_v)

    def device(dy, dx):
        return (lax.rem(by + dy + nby, nby), lax.rem(bx + dx + nbx, nbx))

    loads = [
        pltpu.make_async_copy(src, dst, in_sem.at[i])
        for i, (src, dst) in enumerate(
            [(kmt_in, kmt_v), (temp_in, raw.at[0]), (uvel_in, raw.at[1]), (vvel_in, raw.at[2])]
        )
    ]
    for load in loads:
        load.start()

    barrier = pltpu.get_barrier_semaphore()
    greeted = [device(0, o) for o in range(1, nbx)]
    greeted += [device(d, 0) for d in range(-RADIUS, RADIUS + 1) if d]
    greeted += [device(dy, dx) for dy, dx in DIRS if dy and dx]
    for dev in greeted:
        pl.semaphore_signal(barrier, inc=1, device_id=dev, device_id_type=MESH)

    keep_s = jnp.where(by == 0, F32(0.0), F32(1.0))
    keep_n = jnp.where(by == nby - 1, F32(0.0), F32(1.0))
    lane8 = lanes_of((8, COLS))
    sub8 = lax.broadcasted_iota(jnp.int32, (8, COLS), 0)

    loads[0].wait()
    depth_v[...] = kmt_v[...].astype(F32)
    for f in range(3):
        loads[1 + f].wait()
        pad = pads[f]

        def pack(c, carry, f=f, pad=pad):
            packed = jnp.zeros((8, COLS), F32)
            rows = pad.at[pl.ds(pl.multiple_of(c * (PITCH * CHUNK), PITCH * CHUNK), PITCH * (CHUNK + 2)), :]
            for l in range(CHUNK):
                tile = raw[f, c * CHUNK + l]
                rows[pl.ds(PITCH * (l + 1), 8), :] = tile
                packed = jnp.where(lane8 // 4 == l, roll(tile, 2 + 4 * l, 1), packed)
            quarter = lax.rem(c, 4)
            packed = roll(packed, 32 * quarter, 1)
            half = c // 4
            before = tx_col[2 * f + half]
            tx_col[2 * f + half] = jnp.where(lane8 // 32 == quarter, packed, before)
            return carry

        for half in range(2):
            tx_col[2 * f + half] = jnp.zeros((8, COLS), F32)
        lax.fori_loop(0, KL // CHUNK, pack, 0)
    tx_col[6] = depth_v[...]

    def edge_row(f, row):
        return pads[f][pl.ds(PITCH + row, KL, stride=PITCH), :]

    lane_row = lanes_of((8, COLS))
    for side, (row, inner) in enumerate([(0, 1), (ROWS - 1, ROWS - 2)]):
        edges = [edge_row(f, row) for f in range(3)]
        tx_row1[side, 0:KL] = edges[0]
        tx_row1[side, KL : 2 * KL] = edge_row(0, inner)
        tx_row1[side, 2 * KL : 3 * KL] = edges[1]
        tx_row1[side, 3 * KL : 4 * KL] = edges[2]
        tx_row1[side, 4 * KL : 4 * KL + 8] = depth_v[...]
        tx_row2[side, 0:KL] = edge_row(1, inner)
        tx_row2[side, KL : 2 * KL] = edge_row(2, inner)
        corner = jnp.zeros((8, COLS), F32)
        for f in range(3):
            for g in range(6):
                at = 2 * (6 * f + g)
                corner = jnp.where(lane_row // 2 == at // 2, roll(edges[f][8 * g : 8 * g + 8], 1 + at, 1), corner)
        tx_cor[side, 0:8] = depth_v[...]
        tx_cor[side, 8:16] = corner
        for i in range(6):
            tx_cor[side, 16 + i : 17 + i] = tx_col[i, row : row + 1]
        tx_cor[side, 22:24] = jnp.zeros((2, COLS), F32)

    def remote(src, dst, send, recv, dev):
        return pltpu.make_async_remote_copy(
            src_ref=src, dst_ref=dst, send_sem=send, recv_sem=recv, device_id=dev, device_id_type=MESH
        )

    pl.semaphore_wait(barrier, len(greeted))

    south, north, west, east = device(-1, 0), device(1, 0), device(0, -1), device(0, 1)
    row1 = [
        remote(tx_row1.at[0], rx_row1.at[1], row1_s.at[0], row1_r.at[1], south),
        remote(tx_row1.at[1], rx_row1.at[0], row1_s.at[1], row1_r.at[0], north),
    ]
    cols = [
        remote(tx_col, rx_col.at[1], col_s.at[0], col_r.at[1], west),
        remote(tx_col, rx_col.at[0], col_s.at[1], col_r.at[0], east),
    ]
    diagonal = [SW, SE, NW, NE]
    cors = []
    for i, d in enumerate(diagonal):
        dy, dx = DIRS[d]
        cors.append(
            remote(tx_cor.at[0 if dy < 0 else 1], rx_cor.at[3 - i], cor_s.at[i], cor_r.at[3 - i], device(dy, dx))
        )
    row2 = [
        remote(tx_row2.at[0], rx_row2.at[1], row2_s.at[0], row2_r.at[1], south),
        remote(tx_row2.at[1], rx_row2.at[0], row2_s.at[1], row2_r.at[0], north),
    ]
    first = row1 + cols + cors
    for copy in first + row2:
        copy.start()

    def tell(step, reach):
        for d in (-reach, reach):
            pl.semaphore_signal(known.at[step], inc=1, device_id=device(d, 0), device_id_type=MESH)

    tell(0, RADIUS)

    for star in stars:
        star[0:PITCH, :] = jnp.zeros((PITCH, COLS), F32)
        star[PADDED - PITCH : PADDED, :] = jnp.zeros((PITCH, COLS), F32)

    for copy in first:
        copy.wait_recv()
    pl.semaphore_wait(known.at[0], 2)
    tell(1, 2 * RADIUS)

    dep = {
        S: keep_s * rx_row1[0, 4 * KL : 4 * KL + 8],
        N: keep_n * rx_row1[1, 4 * KL : 4 * KL + 8],
        W: rx_col[0, 6],
        E: rx_col[1, 6],
        SW: keep_s * rx_cor[0, 0:8],
        SE: keep_s * rx_cor[1, 0:8],
        NW: keep_n * rx_cor[2, 0:8],
        NE: keep_n * rx_cor[3, 0:8],
    }

    def patch(own, near):
        beside = jnp.where(lane8 < 64, near[E], near[W])
        below = jnp.where(sub8 < 4, near[N], near[S])
        across = jnp.where(
            sub8 < 4, jnp.where(lane8 < 64, near[NE], near[NW]), jnp.where(lane8 < 64, near[SE], near[SW])
        )
        return jnp.concatenate(
            [jnp.concatenate([own, beside], axis=1), jnp.concatenate([below, across], axis=1)], axis=0
        )

    depth = patch(depth_v[...], dep)
    depths = (depth, roll(depth, -1, 1), roll(depth, 1, 1), roll(depth, -1, 0), roll(depth, 1, 0))
    for i, d in enumerate(depths):
        depths_v[i] = d

    rows1 = {}
    for side, (keep, place) in enumerate([(keep_s, PITCH - 1), (keep_n, PITCH + ROWS)]):
        for f, at in ((0, 0), (1, 2), (2, 3)):
            value = keep * rx_row1[side, at * KL : (at + 1) * KL]
            pads[f][pl.ds(place, KL, stride=PITCH), :] = value
            rows1[side, f] = value

    odd = lane8 % 4 >= 2
    for i in range(6):
        q_ref[i] = jnp.where(odd, rx_col[1, i], rx_col[0, i])
    lane_corner = [
        keep * jnp.where(odd, rx_cor[2 * side + 1, 16:24], rx_cor[2 * side, 16:24])
        for side, keep in enumerate((keep_s, keep_n))
    ]
    level_corner = [
        keep * jnp.where(lane8 % 2 == 1, rx_cor[2 * side + 1, 8:16], rx_cor[2 * side, 8:16])
        for side, keep in enumerate((keep_s, keep_n))
    ]

    level_rows = lax.broadcasted_iota(jnp.int32, (KL, COLS), 0).astype(F32)

    def star_rows(fields, second):
        for side, (row, place) in enumerate([(2 * ROWS - 1, PITCH - 1), (ROWS, PITCH + ROWS)]):
            near = [depths_v[i, row : row + 1, 0:COLS] for i in range(5)]
            terms = star_terms(level_rows, near, rows1[side, 1], rows1[side, 2])
            for f in fields:
                cell = rows1[side, f]
                inner = edge_row(f, 0 if side == 0 else ROWS - 1)
                outer = second(side, f)
                edge = jnp.concatenate(
                    [roll(level_corner[side], COLS - 1 - 2 * (6 * f + g), 1) for g in range(6)], axis=0
                )
                e, w = east_west(cell, edge)
                n, s = (inner, outer) if side == 0 else (outer, inner)
                stars[f][pl.ds(place, KL, stride=PITCH), :] = star_value(terms, cell, (e, w, n, s))

    def star_cols(fields):
        near = [
            jnp.where(odd, depths_v[i, 0:8, COLS : COLS + 1], depths_v[i, 0:8, 2 * COLS - 1 : 2 * COLS]) for i in range(5)
        ]
        for half in range(2):
            level = (lane8 // 4 + 32 * half).astype(F32)
            terms = star_terms(level, near, q_ref[2 + half], q_ref[4 + half])
            for f in fields:
                i = 2 * f + half
                cell, own = q_ref[i], tx_col[i]
                e = jnp.where(odd, roll(cell, -1, 1), roll(own, -1, 1))
                w = jnp.where(odd, roll(own, 1, 1), roll(cell, 1, 1))
                n = jnp.where(sub8 == ROWS - 1, lane_corner[1][i : i + 1], roll(cell, -1, 0))
                s = jnp.where(sub8 == 0, lane_corner[0][i : i + 1], roll(cell, 1, 0))
                qs_ref[i] = star_value(terms, cell, (e, w, n, s))

    def near_own():
        return [depths_v[i, 0:8, 0:COLS] for i in range(5)]

    def chunk_rows(ref, c):
        return ref.at[pl.ds(pl.multiple_of(c * (PITCH * CHUNK), PITCH * CHUNK), PITCH * (CHUNK + 2)), :]

    def edge_of(ref, f, c, l):
        shift = lax.rem(2 * COLS - 2 - 32 * lax.rem(c, 4) - 4 * l, COLS)
        return roll(ref[2 * f + c // 4], shift, 1)

    def star_own(fields):
        def step(c, carry):
            near = near_own()
            views = [chunk_rows(pad, c) for pad in pads]
            outs = [chunk_rows(star, c) for star in stars]
            for l in range(CHUNK):
                base = PITCH * (l + 1)
                level = (c * CHUNK + l).astype(F32)
                terms = star_terms(
                    level, near, views[1][pl.ds(base, 8), :], views[2][pl.ds(base, 8), :]
                )
                for f in fields:
                    cell = views[f][pl.ds(base, 8), :]
                    e, w = east_west(cell, edge_of(q_ref, f, c, l))
                    n = views[f][pl.ds(base + 1, 8), :]
                    s = views[f][pl.ds(base - 1, 8), :]
                    outs[f][pl.ds(base, 8), :] = star_value(terms, cell, (e, w, n, s))
            return carry

        lax.fori_loop(0, KL // CHUNK, step, 0)

    def update_own(fields):
        def step(c, total):
            near = near_own()
            views = [chunk_rows(star, c) for star in stars]
            for l in range(CHUNK):
                base = PITCH * (l + 1)
                level = (c * CHUNK + l).astype(F32)
                smooth = [jnp.where(level < d, F32(STEP_SMOOTH), F32(0.0)) for d in near[1:]]
                up = jnp.where(level + F32(1.0) < near[0], F32(STEP_VERT), F32(0.0))
                down = jnp.where(level > F32(0.0), F32(STEP_VERT), F32(0.0))
                own = F32(1.0) - (((smooth[0] + smooth[1]) + (smooth[2] + smooth[3])) + (up + down))
                centre = level < near[0]
                for f in fields:
                    view = views[f]
                    cell = view[pl.ds(base, 8), :]
                    e, w = east_west(cell, edge_of(qs_ref, f, c, l))
                    n = view[pl.ds(base + 1, 8), :]
                    s = view[pl.ds(base - 1, 8), :]
                    above = view[pl.ds(base + PITCH, 8), :]
                    below = view[pl.ds(base - PITCH, 8), :]
                    value = own * cell + F32(STEP_SMOOTH) * ((e + w) + (n + s)) + F32(STEP_VERT) * (above + below)
                    value = jnp.where(centre, value, F32(0.0))
                    fresh[f, c * CHUNK + l] = value
                    if f == 0:
                        total = total + value
            return total

        return lax.fori_loop(0, KL // CHUNK, step, jnp.zeros((8, COLS), F32))

    star_rows([0], lambda side, f: (keep_s, keep_n)[side] * rx_row1[side, KL : 2 * KL])
    star_cols([0])
    star_own([0])
    rhs = update_own([0]) * F32(1.0 / math.sqrt(KL))

    height = depths_v[0] * F32(1.0 / KL)
    w_e = jnp.minimum(height, roll(height, -1, 1))
    w_n = jnp.minimum(height, roll(height, -1, 0))
    w_w = roll(w_e, 1, 1)
    w_s = roll(w_n, 1, 0)
    diag = F32(SURFACE_TERM) + w_e + w_w + w_n + w_s
    inverse = F32(1.0) / diag
    scaled = (w_e * inverse, w_w * inverse, w_n * inverse, w_s * inverse)

    tx_u[...] = rhs * inverse[0:8, 0:COLS]
    round_u = [
        remote(tx_u, rx_u.at[7 - i], u_s.at[i], u_r.at[7 - i], device(dy, dx)) for i, (dy, dx) in enumerate(DIRS)
    ]
    for copy in round_u:
        copy.start()
    saves = [
        pltpu.make_async_copy(fresh.at[f], dst, out_sem.at[f]) for f, dst in enumerate((temp_out, uvel_out, vvel_out))
    ]
    saves[0].start()
    for copy in round_u:
        copy.wait_recv()
    pl.semaphore_wait(known.at[1], 2)
    tell(2, 4 * RADIUS)

    power = patch(tx_u[...], {d: rx_u[d] for d in range(8)})
    powers = [power]
    for _ in range(ITERS):
        e, w = roll(power, -1, 1), roll(power, 1, 1)
        n, s = roll(power, -1, 0), roll(power, 1, 0)
        power = (scaled[0] * e + scaled[1] * w) + (scaled[2] * n + scaled[3] * s)
        powers.append(power)
    own_diag = diag[0:8, 0:COLS]
    powers = [p[0:8, 0:COLS] for p in powers]
    weighted = [own_diag * p for p in powers]

    row = jnp.zeros((1, COLS), F32)
    lane1 = lanes_of((1, COLS))
    for k, (i, j) in enumerate(GRAM):
        part = jnp.sum(jnp.sum(weighted[i] * powers[j], axis=0, keepdims=True), axis=1, keepdims=True)
        row = jnp.where(lane1 == k, part, row)

    tx_bx[...] = row
    over_bx = [
        remote(tx_bx, rx_bx.at[o - 1], bx_s, bx_r, device(0, o)) for o in range(1, nbx)
    ]
    for copy in over_bx:
        copy.start()
    remote(rx_bx, rx_bx, bx_s, bx_r, east).wait_recv()
    row = row + jnp.sum(rx_bx[...], axis=0)
    pl.semaphore_wait(known.at[2], 2)

    tx_by[...] = row
    order = sorted(range(1, nby), key=lambda o: -min(o, nby - o))
    over_by = [remote(tx_by, rx_by.at[o - 1], by_s, by_r, device(o, 0)) for o in order]
    for copy in over_by:
        copy.start()

    for copy in row2:
        copy.wait_recv()
    star_rows([1, 2], lambda side, f: (keep_s, keep_n)[side] * rx_row2[side, (f - 1) * KL : f * KL])
    star_cols([1, 2])
    star_own([1, 2])
    update_own([1, 2])
    saves[1].start()
    saves[2].start()
    for copy in first + row2 + round_u:
        copy.wait_send()
    remote(rx_bx, rx_bx, bx_s, bx_r, east).wait_send()

    remote(rx_by, rx_by, by_s, by_r, north).wait_recv()
    row = row + jnp.sum(rx_by[...], axis=0)

    gram = {}
    for k, (i, j) in enumerate(GRAM):
        gram[i, j] = gram[j, i] = row[0:1, k : k + 1]

    def inner(a, b):
        total = None
        for i, ai in enumerate(a):
            for j, bj in enumerate(b):
                term = ai * bj * gram[i, j]
                total = term if total is None else total + term
        return total

    one = jnp.ones((1, 1), F32)
    z, p, x = [one], [one], []
    rz = inner(z, z)
    for step in range(ITERS):
        q = [p[0]] + [p[i] - p[i - 1] for i in range(1, len(p))] + [-p[-1]]
        alpha = rz / inner(p, q)
        x = [x[i] + alpha * p[i] if i < len(x) else alpha * p[i] for i in range(len(p))]
        z = [z[i] - alpha * q[i] if i < len(z) else -(alpha * q[i]) for i in range(len(q))]
        if step + 1 < ITERS:
            rz_next = inner(z, z)
            beta = rz_next / rz
            p = [z[i] + beta * p[i] if i < len(p) else z[i] for i in range(len(z))]
            rz = rz_next

    surface = x[0] * powers[0]
    for i in range(1, ITERS):
        surface = surface + x[i] * powers[i]
    resid = z[0] * weighted[0]
    for i in range(1, ITERS + 1):
        resid = resid + z[i] * weighted[i]
    surf_v[...] = surface
    resid_v[...] = resid
    saves.append(pltpu.make_async_copy(surf_v, surface_out, out_sem.at[3]))
    saves.append(pltpu.make_async_copy(resid_v, resid_out, out_sem.at[4]))
    saves[3].start()
    saves[4].start()
    remote(rx_by, rx_by, by_s, by_r, north).wait_send()
    for save in saves:
        save.wait()


def solution(mesh):
    nby, nbx = mesh.shape["by"], mesh.shape["bx"]

    def on_device(temp, uvel, vvel, kmt):
        field = jax.ShapeDtypeStruct(temp.shape, F32)
        plane = jax.ShapeDtypeStruct(kmt.shape, F32)
        vmem, dma = pltpu.VMEM, pltpu.SemaphoreType.DMA
        return pl.pallas_call(
            lambda *refs: kernel(nby, nbx, *refs),
            out_shape=(field, field, field, plane, plane),
            in_specs=[pl.BlockSpec(memory_space=pl.ANY)] * 4,
            out_specs=(pl.BlockSpec(memory_space=pl.ANY),) * 5,
            scratch_shapes=[
                vmem((3, KL, ROWS, COLS), F32),
                vmem((ROWS, COLS), jnp.int32),
                *[vmem((PADDED, COLS), F32)] * 6,
                vmem((3, KL, ROWS, COLS), F32),
                vmem((ROWS, COLS), F32),
                vmem((ROWS, COLS), F32),
                vmem((ROWS, COLS), F32),
                vmem((5, 2 * ROWS, 2 * COLS), F32),
                vmem((6, ROWS, COLS), F32),
                vmem((6, ROWS, COLS), F32),
                vmem((2, 4 * KL + 8, COLS), F32),
                vmem((2, 2 * KL, COLS), F32),
                vmem((7, ROWS, COLS), F32),
                vmem((2, 24, COLS), F32),
                vmem((2, 4 * KL + 8, COLS), F32),
                vmem((2, 2 * KL, COLS), F32),
                vmem((2, 7, ROWS, COLS), F32),
                vmem((4, 24, COLS), F32),
                vmem((ROWS, COLS), F32),
                vmem((8, ROWS, COLS), F32),
                vmem((1, COLS), F32),
                vmem((nbx - 1, 1, COLS), F32),
                vmem((1, COLS), F32),
                vmem((nby - 1, 1, COLS), F32),
                dma((4,)), dma((5,)),
                dma((2,)), dma((2,)), dma((2,)), dma((2,)),
                dma((2,)), dma((2,)), dma((4,)), dma((4,)),
                dma((8,)), dma((8,)),
                dma, dma, dma, dma,
                pltpu.SemaphoreType.REGULAR((3,)),
            ],
            compiler_params=pltpu.CompilerParams(
                collective_id=0, has_side_effects=True, vmem_limit_bytes=32 * 1024 * 1024
            ),
        )(temp, uvel, vvel, kmt)

    in_specs = (P(None, "by", "bx"), P(None, "by", "bx"), P(None, "by", "bx"), P("by", "bx"))
    out_specs = (
        P(None, "by", "bx"),
        P(None, "by", "bx"),
        P(None, "by", "bx"),
        P("by", "bx"),
        P("by", "bx"),
    )
    return jax.shard_map(on_device, mesh=mesh, in_specs=in_specs, out_specs=out_specs, check_vma=False)
```

```python
import math

import jax
import jax.numpy as jnp
from jax import lax
from jax.experimental import pallas as pl
from jax.experimental.pallas import tpu as pltpu
from jax.sharding import PartitionSpec as P

ITERS = 3
STEP_DIFF = 0.1
STEP_ADV = 0.5
STEP_SMOOTH = 0.1
STEP_VERT = 0.2
SURFACE_TERM = 0.25

KL, ROWS, COLS = 48, 8, 128
CHUNK = 8
PITCH = 16
PADDED = PITCH * (KL + 2)
RADIUS = 4

F32 = jnp.float32
MESH = pl.DeviceIdType.MESH

DIRS = [(-1, -1), (-1, 0), (-1, 1), (0, -1), (0, 1), (1, -1), (1, 0), (1, 1)]
SW, S, SE, W, E, NW, N, NE = range(8)

GRAM = [(i, j) for i in range(ITERS + 1) for j in range(i, ITERS + 1)]


def roll(value, shift, axis):
    size = value.shape[axis]
    return pltpu.roll(value, shift % size if isinstance(shift, int) else shift, axis)


def lanes_of(shape):
    return lax.broadcasted_iota(jnp.int32, shape, len(shape) - 1)


def east_west(value, edge):
    lane = lanes_of(value.shape)
    axis = value.ndim - 1
    east = roll(jnp.where(lane == 0, edge, value), -1, axis)
    west = roll(jnp.where(lane == COLS - 1, edge, value), 1, axis)
    return east, west


def star_terms(level, depths, uvel, vvel):
    centre = level < depths[0]
    diff = [jnp.where(level < d, F32(STEP_DIFF), F32(0.0)) for d in depths[1:]]
    own = F32(1.0) - ((diff[0] + diff[1]) + (diff[2] + diff[3]))
    adv_u = F32(0.5 * STEP_ADV) * uvel
    adv_v = F32(0.5 * STEP_ADV) * vvel
    return centre, own, (diff[0] - adv_u, diff[1] + adv_u, diff[2] - adv_v, diff[3] + adv_v)


def star_value(terms, cell, sides):
    centre, own, factors = terms
    total = own * cell
    for factor, side in zip(factors, sides):
        total = total + factor * side
    return jnp.where(centre, total, F32(0.0))


def kernel(
    nby, nbx,
    temp_in, uvel_in, vvel_in, kmt_in,
    temp_out, uvel_out, vvel_out, surface_out, resid_out,
    raw, kmt_v, pad_t, pad_u, pad_v, star_t, star_u, star_v, depth_v, depths_v, q_ref, qs_ref,
    tx_row1, tx_row2, tx_col, tx_cor, rx_row1, rx_row2, rx_col, rx_cor,
    tx_u, rx_u, tx_bx, rx_bx, tx_by, rx_by,
    in_sem, row1_s, row1_r, row2_s, row2_r, col_s, col_r, cor_s, cor_r, u_s, u_r, bx_s, bx_r, by_s, by_r,
    known,
):
    by, bx = lax.axis_index("by"), lax.axis_index("bx")
    pads = (pad_t, pad_u, pad_v)
    stars = (star_t, star_u, star_v)
    fresh = (temp_out, uvel_out, vvel_out)

    def device(dy, dx):
        return (lax.rem(by + dy + nby, nby), lax.rem(bx + dx + nbx, nbx))

    loads = [
        pltpu.make_async_copy(src, dst, in_sem.at[i])
        for i, (src, dst) in enumerate(
            [(kmt_in, kmt_v), (temp_in, raw.at[0]), (uvel_in, raw.at[1]), (vvel_in, raw.at[2])]
        )
    ]
    for load in loads:
        load.start()

    barrier = pltpu.get_barrier_semaphore()
    greeted = [device(0, o) for o in range(1, nbx)]
    greeted += [device(d, 0) for d in range(-RADIUS, RADIUS + 1) if d]
    greeted += [device(dy, dx) for dy, dx in DIRS if dy and dx]
    for dev in greeted:
        pl.semaphore_signal(barrier, inc=1, device_id=dev, device_id_type=MESH)

    keep_s = jnp.where(by == 0, F32(0.0), F32(1.0))
    keep_n = jnp.where(by == nby - 1, F32(0.0), F32(1.0))
    lane8 = lanes_of((8, COLS))
    sub8 = lax.broadcasted_iota(jnp.int32, (8, COLS), 0)

    loads[0].wait()
    depth_v[...] = kmt_v[...].astype(F32)
    for f in range(3):
        loads[1 + f].wait()
        pad = pads[f]

        def pack(c, carry, f=f, pad=pad):
            packed = jnp.zeros((8, COLS), F32)
            rows = pad.at[pl.ds(pl.multiple_of(c * (PITCH * CHUNK), PITCH * CHUNK), PITCH * (CHUNK + 2)), :]
            for l in range(CHUNK):
                tile = raw[f, c * CHUNK + l]
                rows[pl.ds(PITCH * (l + 1), 8), :] = tile
                packed = jnp.where(lane8 // 4 == l, roll(tile, 2 + 4 * l, 1), packed)
            quarter = lax.rem(c, 4)
            packed = roll(packed, 32 * quarter, 1)
            half = c // 4
            before = tx_col[2 * f + half]
            tx_col[2 * f + half] = jnp.where(lane8 // 32 == quarter, packed, before)
            return carry

        for half in range(2):
            tx_col[2 * f + half] = jnp.zeros((8, COLS), F32)
        lax.fori_loop(0, KL // CHUNK, pack, 0)
    tx_col[6] = depth_v[...]

    def edge_row(f, row):
        return pads[f][pl.ds(PITCH + row, KL, stride=PITCH), :]

    lane_row = lanes_of((8, COLS))
    for side, (row, inner) in enumerate([(0, 1), (ROWS - 1, ROWS - 2)]):
        edges = [edge_row(f, row) for f in range(3)]
        tx_row1[side, 0:KL] = edges[0]
        tx_row1[side, KL : 2 * KL] = edge_row(0, inner)
        tx_row1[side, 2 * KL : 3 * KL] = edges[1]
        tx_row1[side, 3 * KL : 4 * KL] = edges[2]
        tx_row1[side, 4 * KL : 4 * KL + 8] = depth_v[...]
        tx_row2[side, 0:KL] = edge_row(1, inner)
        tx_row2[side, KL : 2 * KL] = edge_row(2, inner)
        corner = jnp.zeros((8, COLS), F32)
        for f in range(3):
            for g in range(6):
                at = 2 * (6 * f + g)
                corner = jnp.where(lane_row // 2 == at // 2, roll(edges[f][8 * g : 8 * g + 8], 1 + at, 1), corner)
        tx_cor[side, 0:8] = depth_v[...]
        tx_cor[side, 8:16] = corner
        for i in range(6):
            tx_cor[side, 16 + i : 17 + i] = tx_col[i, row : row + 1]
        tx_cor[side, 22:24] = jnp.zeros((2, COLS), F32)

    def remote(src, dst, send, recv, dev):
        return pltpu.make_async_remote_copy(
            src_ref=src, dst_ref=dst, send_sem=send, recv_sem=recv, device_id=dev, device_id_type=MESH
        )

    pl.semaphore_wait(barrier, len(greeted))

    south, north, west, east = device(-1, 0), device(1, 0), device(0, -1), device(0, 1)
    row1 = [
        remote(tx_row1.at[0], rx_row1.at[1], row1_s.at[0], row1_r.at[1], south),
        remote(tx_row1.at[1], rx_row1.at[0], row1_s.at[1], row1_r.at[0], north),
    ]
    cols = [
        remote(tx_col, rx_col.at[1], col_s.at[0], col_r.at[1], west),
        remote(tx_col, rx_col.at[0], col_s.at[1], col_r.at[0], east),
    ]
    diagonal = [SW, SE, NW, NE]
    cors = []
    for i, d in enumerate(diagonal):
        dy, dx = DIRS[d]
        cors.append(
            remote(tx_cor.at[0 if dy < 0 else 1], rx_cor.at[3 - i], cor_s.at[i], cor_r.at[3 - i], device(dy, dx))
        )
    row2 = [
        remote(tx_row2.at[0], rx_row2.at[1], row2_s.at[0], row2_r.at[1], south),
        remote(tx_row2.at[1], rx_row2.at[0], row2_s.at[1], row2_r.at[0], north),
    ]
    first = row1 + cols + cors
    for copy in first + row2:
        copy.start()

    def tell(step, reach):
        for d in (-reach, reach):
            pl.semaphore_signal(known.at[step], inc=1, device_id=device(d, 0), device_id_type=MESH)

    tell(0, RADIUS)

    for star in stars:
        star[0:PITCH, :] = jnp.zeros((PITCH, COLS), F32)
        star[PADDED - PITCH : PADDED, :] = jnp.zeros((PITCH, COLS), F32)

    for copy in first:
        copy.wait_recv()
    pl.semaphore_wait(known.at[0], 2)
    tell(1, 2 * RADIUS)

    dep = {
        S: keep_s * rx_row1[0, 4 * KL : 4 * KL + 8],
        N: keep_n * rx_row1[1, 4 * KL : 4 * KL + 8],
        W: rx_col[0, 6],
        E: rx_col[1, 6],
        SW: keep_s * rx_cor[0, 0:8],
        SE: keep_s * rx_cor[1, 0:8],
        NW: keep_n * rx_cor[2, 0:8],
        NE: keep_n * rx_cor[3, 0:8],
    }

    def patch(own, near):
        beside = jnp.where(lane8 < 64, near[E], near[W])
        below = jnp.where(sub8 < 4, near[N], near[S])
        across = jnp.where(
            sub8 < 4, jnp.where(lane8 < 64, near[NE], near[NW]), jnp.where(lane8 < 64, near[SE], near[SW])
        )
        return jnp.concatenate(
            [jnp.concatenate([own, beside], axis=1), jnp.concatenate([below, across], axis=1)], axis=0
        )

    depth = patch(depth_v[...], dep)
    depths = (depth, roll(depth, -1, 1), roll(depth, 1, 1), roll(depth, -1, 0), roll(depth, 1, 0))
    for i, d in enumerate(depths):
        depths_v[i] = d

    rows1 = {}
    for side, (keep, place) in enumerate([(keep_s, PITCH - 1), (keep_n, PITCH + ROWS)]):
        for f, at in ((0, 0), (1, 2), (2, 3)):
            value = keep * rx_row1[side, at * KL : (at + 1) * KL]
            pads[f][pl.ds(place, KL, stride=PITCH), :] = value
            rows1[side, f] = value

    odd = lane8 % 4 >= 2
    for i in range(6):
        q_ref[i] = jnp.where(odd, rx_col[1, i], rx_col[0, i])
    lane_corner = [
        keep * jnp.where(odd, rx_cor[2 * side + 1, 16:24], rx_cor[2 * side, 16:24])
        for side, keep in enumerate((keep_s, keep_n))
    ]
    level_corner = [
        keep * jnp.where(lane8 % 2 == 1, rx_cor[2 * side + 1, 8:16], rx_cor[2 * side, 8:16])
        for side, keep in enumerate((keep_s, keep_n))
    ]

    level_rows = lax.broadcasted_iota(jnp.int32, (KL, COLS), 0).astype(F32)

    def star_rows(fields, second):
        for side, (row, place) in enumerate([(2 * ROWS - 1, PITCH - 1), (ROWS, PITCH + ROWS)]):
            near = [depths_v[i, row : row + 1, 0:COLS] for i in range(5)]
            terms = star_terms(level_rows, near, rows1[side, 1], rows1[side, 2])
            for f in fields:
                cell = rows1[side, f]
                inner = edge_row(f, 0 if side == 0 else ROWS - 1)
                outer = second(side, f)
                edge = jnp.concatenate(
                    [roll(level_corner[side], COLS - 1 - 2 * (6 * f + g), 1) for g in range(6)], axis=0
                )
                e, w = east_west(cell, edge)
                n, s = (inner, outer) if side == 0 else (outer, inner)
                stars[f][pl.ds(place, KL, stride=PITCH), :] = star_value(terms, cell, (e, w, n, s))

    def star_cols(fields):
        near = [
            jnp.where(odd, depths_v[i, 0:8, COLS : COLS + 1], depths_v[i, 0:8, 2 * COLS - 1 : 2 * COLS]) for i in range(5)
        ]
        for half in range(2):
            level = (lane8 // 4 + 32 * half).astype(F32)
            terms = star_terms(level, near, q_ref[2 + half], q_ref[4 + half])
            for f in fields:
                i = 2 * f + half
                cell, own = q_ref[i], tx_col[i]
                e = jnp.where(odd, roll(cell, -1, 1), roll(own, -1, 1))
                w = jnp.where(odd, roll(own, 1, 1), roll(cell, 1, 1))
                n = jnp.where(sub8 == ROWS - 1, lane_corner[1][i : i + 1], roll(cell, -1, 0))
                s = jnp.where(sub8 == 0, lane_corner[0][i : i + 1], roll(cell, 1, 0))
                qs_ref[i] = star_value(terms, cell, (e, w, n, s))

    def near_own():
        return [depths_v[i, 0:8, 0:COLS] for i in range(5)]

    def chunk_rows(ref, c):
        return ref.at[pl.ds(pl.multiple_of(c * (PITCH * CHUNK), PITCH * CHUNK), PITCH * (CHUNK + 2)), :]

    def edge_of(ref, f, c, l):
        shift = lax.rem(2 * COLS - 2 - 32 * lax.rem(c, 4) - 4 * l, COLS)
        return roll(ref[2 * f + c // 4], shift, 1)

    def star_own(fields):
        def step(c, carry):
            near = near_own()
            views = [chunk_rows(pad, c) for pad in pads]
            outs = [chunk_rows(star, c) for star in stars]
            for l in range(CHUNK):
                base = PITCH * (l + 1)
                level = (c * CHUNK + l).astype(F32)
                terms = star_terms(
                    level, near, views[1][pl.ds(base, 8), :], views[2][pl.ds(base, 8), :]
                )
                for f in fields:
                    cell = views[f][pl.ds(base, 8), :]
                    e, w = east_west(cell, edge_of(q_ref, f, c, l))
                    n = views[f][pl.ds(base + 1, 8), :]
                    s = views[f][pl.ds(base - 1, 8), :]
                    outs[f][pl.ds(base, 8), :] = star_value(terms, cell, (e, w, n, s))
            return carry

        lax.fori_loop(0, KL // CHUNK, step, 0)

    def update_own(fields):
        def step(c, total):
            near = near_own()
            views = [chunk_rows(star, c) for star in stars]
            for l in range(CHUNK):
                base = PITCH * (l + 1)
                level = (c * CHUNK + l).astype(F32)
                smooth = [jnp.where(level < d, F32(STEP_SMOOTH), F32(0.0)) for d in near[1:]]
                up = jnp.where(level + F32(1.0) < near[0], F32(STEP_VERT), F32(0.0))
                down = jnp.where(level > F32(0.0), F32(STEP_VERT), F32(0.0))
                own = F32(1.0) - (((smooth[0] + smooth[1]) + (smooth[2] + smooth[3])) + (up + down))
                centre = level < near[0]
                for f in fields:
                    view = views[f]
                    cell = view[pl.ds(base, 8), :]
                    e, w = east_west(cell, edge_of(qs_ref, f, c, l))
                    n = view[pl.ds(base + 1, 8), :]
                    s = view[pl.ds(base - 1, 8), :]
                    above = view[pl.ds(base + PITCH, 8), :]
                    below = view[pl.ds(base - PITCH, 8), :]
                    value = own * cell + F32(STEP_SMOOTH) * ((e + w) + (n + s)) + F32(STEP_VERT) * (above + below)
                    value = jnp.where(centre, value, F32(0.0))
                    fresh[f][c * CHUNK + l] = value
                    if f == 0:
                        total = total + value
            return total

        return lax.fori_loop(0, KL // CHUNK, step, jnp.zeros((8, COLS), F32))

    star_rows([0], lambda side, f: (keep_s, keep_n)[side] * rx_row1[side, KL : 2 * KL])
    star_cols([0])
    star_own([0])
    rhs = update_own([0]) * F32(1.0 / math.sqrt(KL))

    height = depths_v[0] * F32(1.0 / KL)
    w_e = jnp.minimum(height, roll(height, -1, 1))
    w_n = jnp.minimum(height, roll(height, -1, 0))
    w_w = roll(w_e, 1, 1)
    w_s = roll(w_n, 1, 0)
    diag = F32(SURFACE_TERM) + w_e + w_w + w_n + w_s
    inverse = F32(1.0) / diag
    scaled = (w_e * inverse, w_w * inverse, w_n * inverse, w_s * inverse)

    tx_u[...] = rhs * inverse[0:8, 0:COLS]
    round_u = [
        remote(tx_u, rx_u.at[7 - i], u_s.at[i], u_r.at[7 - i], device(dy, dx)) for i, (dy, dx) in enumerate(DIRS)
    ]
    for copy in round_u:
        copy.start()
    for copy in round_u:
        copy.wait_recv()
    pl.semaphore_wait(known.at[1], 2)
    tell(2, 4 * RADIUS)

    power = patch(tx_u[...], {d: rx_u[d] for d in range(8)})
    powers = [power]
    for _ in range(ITERS):
        e, w = roll(power, -1, 1), roll(power, 1, 1)
        n, s = roll(power, -1, 0), roll(power, 1, 0)
        power = (scaled[0] * e + scaled[1] * w) + (scaled[2] * n + scaled[3] * s)
        powers.append(power)
    own_diag = diag[0:8, 0:COLS]
    powers = [p[0:8, 0:COLS] for p in powers]
    weighted = [own_diag * p for p in powers]

    row = jnp.zeros((1, COLS), F32)
    lane1 = lanes_of((1, COLS))
    for k, (i, j) in enumerate(GRAM):
        part = jnp.sum(jnp.sum(weighted[i] * powers[j], axis=0, keepdims=True), axis=1, keepdims=True)
        row = jnp.where(lane1 == k, part, row)

    tx_bx[...] = row
    over_bx = [
        remote(tx_bx, rx_bx.at[o - 1], bx_s, bx_r, device(0, o)) for o in range(1, nbx)
    ]
    for copy in over_bx:
        copy.start()
    remote(rx_bx, rx_bx, bx_s, bx_r, east).wait_recv()
    row = row + jnp.sum(rx_bx[...], axis=0)
    pl.semaphore_wait(known.at[2], 2)

    tx_by[...] = row
    order = sorted(range(1, nby), key=lambda o: -min(o, nby - o))
    over_by = [remote(tx_by, rx_by.at[o - 1], by_s, by_r, device(o, 0)) for o in order]
    for copy in over_by:
        copy.start()

    for copy in row2:
        copy.wait_recv()
    star_rows([1, 2], lambda side, f: (keep_s, keep_n)[side] * rx_row2[side, (f - 1) * KL : f * KL])
    star_cols([1, 2])
    star_own([1, 2])
    update_own([1, 2])
    for copy in first + row2 + round_u:
        copy.wait_send()
    remote(rx_bx, rx_bx, bx_s, bx_r, east).wait_send()

    remote(rx_by, rx_by, by_s, by_r, north).wait_recv()
    row = row + jnp.sum(rx_by[...], axis=0)

    gram = {}
    for k, (i, j) in enumerate(GRAM):
        gram[i, j] = gram[j, i] = row[0:1, k : k + 1]

    def inner(a, b):
        total = None
        for i, ai in enumerate(a):
            for j, bj in enumerate(b):
                term = ai * bj * gram[i, j]
                total = term if total is None else total + term
        return total

    one = jnp.ones((1, 1), F32)
    z, p, x = [one], [one], []
    rz = inner(z, z)
    for step in range(ITERS):
        q = [p[0]] + [p[i] - p[i - 1] for i in range(1, len(p))] + [-p[-1]]
        alpha = rz / inner(p, q)
        x = [x[i] + alpha * p[i] if i < len(x) else alpha * p[i] for i in range(len(p))]
        z = [z[i] - alpha * q[i] if i < len(z) else -(alpha * q[i]) for i in range(len(q))]
        if step + 1 < ITERS:
            rz_next = inner(z, z)
            beta = rz_next / rz
            p = [z[i] + beta * p[i] if i < len(p) else z[i] for i in range(len(z))]
            rz = rz_next

    surface = x[0] * powers[0]
    for i in range(1, ITERS):
        surface = surface + x[i] * powers[i]
    resid = z[0] * weighted[0]
    for i in range(1, ITERS + 1):
        resid = resid + z[i] * weighted[i]
    surface_out[...] = surface
    resid_out[...] = resid
    remote(rx_by, rx_by, by_s, by_r, north).wait_send()


def store(*refs):
    sources, targets, sems = refs[:5], refs[5:10], refs[10]
    copies = [pltpu.make_async_copy(src, dst, sems.at[i]) for i, (src, dst) in enumerate(zip(sources, targets))]
    for copy in copies:
        copy.start()
    for copy in copies:
        copy.wait()


def solution(mesh):
    nby, nbx = mesh.shape["by"], mesh.shape["bx"]

    def on_device(temp, uvel, vvel, kmt):
        field = jax.ShapeDtypeStruct(temp.shape, F32)
        plane = jax.ShapeDtypeStruct(kmt.shape, F32)
        vmem, dma = pltpu.VMEM, pltpu.SemaphoreType.DMA
        results = pl.pallas_call(
            lambda *refs: kernel(nby, nbx, *refs),
            out_shape=(*[pltpu.VMEM(temp.shape, F32)] * 3, *[pltpu.VMEM(kmt.shape, F32)] * 2),
            in_specs=[pl.BlockSpec(memory_space=pltpu.HBM)] * 4,
            out_specs=(pl.BlockSpec(memory_space=pltpu.VMEM),) * 5,
            scratch_shapes=[
                vmem((3, KL, ROWS, COLS), F32),
                vmem((ROWS, COLS), jnp.int32),
                *[vmem((PADDED, COLS), F32)] * 6,
                vmem((ROWS, COLS), F32),
                vmem((5, 2 * ROWS, 2 * COLS), F32),
                vmem((6, ROWS, COLS), F32),
                vmem((6, ROWS, COLS), F32),
                vmem((2, 4 * KL + 8, COLS), F32),
                vmem((2, 2 * KL, COLS), F32),
                vmem((7, ROWS, COLS), F32),
                vmem((2, 24, COLS), F32),
                vmem((2, 4 * KL + 8, COLS), F32),
                vmem((2, 2 * KL, COLS), F32),
                vmem((2, 7, ROWS, COLS), F32),
                vmem((4, 24, COLS), F32),
                vmem((ROWS, COLS), F32),
                vmem((8, ROWS, COLS), F32),
                vmem((1, COLS), F32),
                vmem((nbx - 1, 1, COLS), F32),
                vmem((1, COLS), F32),
                vmem((nby - 1, 1, COLS), F32),
                dma((4,)),
                dma((2,)), dma((2,)), dma((2,)), dma((2,)),
                dma((2,)), dma((2,)), dma((4,)), dma((4,)),
                dma((8,)), dma((8,)),
                dma, dma, dma, dma,
                pltpu.SemaphoreType.REGULAR((3,)),
            ],
            compiler_params=pltpu.CompilerParams(
                collective_id=0, has_side_effects=True, vmem_limit_bytes=32 * 1024 * 1024
            ),
        )(*[pltpu.with_memory_space_constraint(a, pltpu.HBM) for a in (temp, uvel, vvel, kmt)])
        return pl.pallas_call(
            store,
            out_shape=(field, field, field, plane, plane),
            in_specs=[pl.BlockSpec(memory_space=pltpu.VMEM)] * 5,
            out_specs=(pl.BlockSpec(memory_space=pltpu.HBM),) * 5,
            scratch_shapes=[dma((5,))],
            name="store",
        )(*[pltpu.with_memory_space_constraint(r, pltpu.VMEM) for r in results])

    in_specs = (P(None, "by", "bx"), P(None, "by", "bx"), P(None, "by", "bx"), P("by", "bx"))
    out_specs = (
        P(None, "by", "bx"),
        P(None, "by", "bx"),
        P(None, "by", "bx"),
        P("by", "bx"),
        P("by", "bx"),
    )
    return jax.shard_map(on_device, mesh=mesh, in_specs=in_specs, out_specs=out_specs, check_vma=False)
```

```python
import math

import jax
import jax.numpy as jnp
from jax import lax
from jax.experimental import pallas as pl
from jax.experimental.pallas import tpu as pltpu
from jax.sharding import PartitionSpec as P

ITERS = 3
STEP_DIFF = 0.1
STEP_ADV = 0.5
STEP_SMOOTH = 0.1
STEP_VERT = 0.2
SURFACE_TERM = 0.25

KL, ROWS, COLS = 48, 8, 128
CHUNK = 8
PITCH = 16
PADDED = PITCH * (KL + 2)
RADIUS = 4
WIDTH = 4

F32 = jnp.float32
MESH = pl.DeviceIdType.MESH

DIRS = [(-1, -1), (-1, 0), (-1, 1), (0, -1), (0, 1), (1, -1), (1, 0), (1, 1)]
SW, S, SE, W, E, NW, N, NE = range(8)

GRAM = [(i, j) for i in range(ITERS + 1) for j in range(i, ITERS + 1)]


def roll(value, shift, axis):
    size = value.shape[axis]
    return pltpu.roll(value, shift % size if isinstance(shift, int) else shift, axis)


def lanes_of(shape):
    return lax.broadcasted_iota(jnp.int32, shape, len(shape) - 1)


def east_west(value, edge):
    lane = lanes_of(value.shape)
    axis = value.ndim - 1
    east = roll(jnp.where(lane == 0, edge, value), -1, axis)
    west = roll(jnp.where(lane == COLS - 1, edge, value), 1, axis)
    return east, west


def star_terms(level, depths, uvel, vvel):
    centre = level < depths[0]
    diff = [jnp.where(level < d, F32(STEP_DIFF), F32(0.0)) for d in depths[1:]]
    own = F32(1.0) - ((diff[0] + diff[1]) + (diff[2] + diff[3]))
    adv_u = F32(0.5 * STEP_ADV) * uvel
    adv_v = F32(0.5 * STEP_ADV) * vvel
    return centre, own, (diff[0] - adv_u, diff[1] + adv_u, diff[2] - adv_v, diff[3] + adv_v)


def star_value(terms, cell, sides):
    centre, own, factors = terms
    total = own * cell
    for factor, side in zip(factors, sides):
        total = total + factor * side
    return jnp.where(centre, total, F32(0.0))


def two_sum(a, b):
    head = a + b
    shift = head - a
    return head, (a - (head - shift)) + (b - shift)


def quick_sum(a, b):
    head = a + b
    return head, b - (head - a)


def halves(a):
    wide = a * F32(4097.0)
    head = wide - (wide - a)
    return head, a - head


def two_prod(a, b):
    head = a * b
    (ah, al), (bh, bl) = halves(a), halves(b)
    return head, ((ah * bh - head) + ah * bl + al * bh) + al * bl


def add2(a, b):
    head, tail = two_sum(a[0], b[0])
    return quick_sum(head, tail + (a[1] + b[1]))


def sub2(a, b):
    return add2(a, (-b[0], -b[1]))


def minor(a, b, c, d):
    one, one_tail = two_prod(a[0], b[0])
    two, two_tail = two_prod(c[0], d[0])
    value, lost = two_sum(one, -two)
    one_tail = one_tail + (a[0] * b[1] + a[1] * b[0])
    return value + (lost + (one_tail - (two_tail + (c[0] * d[1] + c[1] * d[0]))))


def sum_rows(tiles):
    sub = lax.broadcasted_iota(jnp.int32, (8, COLS), 0)
    for shift in (1, 2, 4):
        mine = sub % (2 * shift) < shift
        tiles = [
            jnp.where(mine, one, other) + roll(jnp.where(mine, other, one), shift, 0)
            for one, other in zip(tiles[0::2], tiles[1::2])
        ]
    return tiles


def add_exact(rows):
    terms = [(row, None) for row in rows]
    while len(terms) > 1:
        paired = []
        for (a, lost_a), (b, lost_b) in zip(terms[0::2], terms[1::2]):
            head, lost = two_sum(a, b)
            for more in (lost_a, lost_b):
                lost = lost if more is None else lost + more
            paired.append((head, lost))
        terms = paired + ([terms[-1]] if len(terms) % 2 else [])
    total, lost = terms[0]
    return total, jnp.zeros_like(total) if lost is None else lost


def kernel(
    nby, nbx,
    temp_in, uvel_in, vvel_in, kmt_in,
    temp_out, uvel_out, vvel_out, surface_out, resid_out,
    raw, kmt_v, pad_t, pad_u, pad_v, star_t, star_u, star_v, depth_v, depths_v, q_ref, qs_ref,
    tx_row1, tx_row2, tx_col, tx_cor, rx_row1, rx_row2, rx_col, rx_cor,
    tx_u, rx_u, tx_bx, rx_bx, tx_by, rx_by,
    in_sem, row1_s, row1_r, row2_s, row2_r, col_s, col_r, cor_s, cor_r, u_s, u_r, bx_s, bx_r, by_s, by_r,
    known,
):
    by, bx = lax.axis_index("by"), lax.axis_index("bx")
    pads = (pad_t, pad_u, pad_v)
    stars = (star_t, star_u, star_v)
    fresh = (temp_out, uvel_out, vvel_out)

    def device(dy, dx):
        return (lax.rem(by + dy + nby, nby), lax.rem(bx + dx + nbx, nbx))

    loads = [
        pltpu.make_async_copy(src, dst, in_sem.at[i])
        for i, (src, dst) in enumerate(
            [(kmt_in, kmt_v), (temp_in, raw.at[0]), (uvel_in, raw.at[1]), (vvel_in, raw.at[2])]
        )
    ]
    for load in loads:
        load.start()

    barrier = pltpu.get_barrier_semaphore()
    across = lax.rem(bx, WIDTH)
    line = bx - across
    plane = [
        (by, line + lax.rem(across + 1, WIDTH)),
        (by, line + lax.rem(across + WIDTH - 1, WIDTH)),
        device(0, WIDTH),
        device(0, -WIDTH),
    ]
    greeted = [device(dy, dx) for dy, dx in DIRS if dx]
    greeted += [device(d, 0) for d in range(-RADIUS, RADIUS + 1) if d]
    greeted += plane
    for dev in greeted:
        pl.semaphore_signal(barrier, inc=1, device_id=dev, device_id_type=MESH)

    keep_s = jnp.where(by == 0, F32(0.0), F32(1.0))
    keep_n = jnp.where(by == nby - 1, F32(0.0), F32(1.0))
    lane8 = lanes_of((8, COLS))
    sub8 = lax.broadcasted_iota(jnp.int32, (8, COLS), 0)

    loads[0].wait()
    depth_v[...] = kmt_v[...].astype(F32)
    for f in range(3):
        loads[1 + f].wait()
        pad = pads[f]

        quads = []
        for c in range(KL // CHUNK):
            packed = jnp.zeros((8, COLS), F32)
            for l in range(CHUNK):
                k = c * CHUNK + l
                tile = raw[f, k]
                pad[PITCH * (k + 1) : PITCH * (k + 1) + 8, :] = tile
                packed = jnp.where(lane8 // 4 == k % 32, roll(tile, 2 + 4 * (k % 32), 1), packed)
            quads.append(packed)
        tx_col[2 * f] = (quads[0] + quads[1]) + (quads[2] + quads[3])
        tx_col[2 * f + 1] = quads[4] + quads[5]
    tx_col[6] = depth_v[...]

    def edge_row(f, row):
        return pads[f][pl.ds(PITCH + row, KL, stride=PITCH), :]

    lane_row = lanes_of((8, COLS))
    for side, (row, inner) in enumerate([(0, 1), (ROWS - 1, ROWS - 2)]):
        edges = [edge_row(f, row) for f in range(3)]
        tx_row1[side, 0:KL] = edges[0]
        tx_row1[side, KL : 2 * KL] = edge_row(0, inner)
        tx_row1[side, 2 * KL : 3 * KL] = edges[1]
        tx_row1[side, 3 * KL : 4 * KL] = edges[2]
        tx_row1[side, 4 * KL : 4 * KL + 8] = depth_v[...]
        tx_row2[side, 0:KL] = edge_row(1, inner)
        tx_row2[side, KL : 2 * KL] = edge_row(2, inner)
        corner = jnp.zeros((8, COLS), F32)
        for f in range(3):
            for g in range(6):
                at = 2 * (6 * f + g)
                corner = jnp.where(lane_row // 2 == at // 2, roll(edges[f][8 * g : 8 * g + 8], 1 + at, 1), corner)
        tx_cor[side, 0:8] = depth_v[...]
        tx_cor[side, 8:16] = corner
        for i in range(6):
            tx_cor[side, 16 + i : 17 + i] = tx_col[i, row : row + 1]
        tx_cor[side, 22:24] = jnp.zeros((2, COLS), F32)

    def remote(src, dst, send, recv, dev):
        return pltpu.make_async_remote_copy(
            src_ref=src, dst_ref=dst, send_sem=send, recv_sem=recv, device_id=dev, device_id_type=MESH
        )

    pl.semaphore_wait(barrier, len(greeted))

    south, north, west, east = device(-1, 0), device(1, 0), device(0, -1), device(0, 1)
    row1 = [
        remote(tx_row1.at[0], rx_row1.at[1], row1_s.at[0], row1_r.at[1], south),
        remote(tx_row1.at[1], rx_row1.at[0], row1_s.at[1], row1_r.at[0], north),
    ]
    cols = [
        remote(tx_col, rx_col.at[1], col_s.at[0], col_r.at[1], west),
        remote(tx_col, rx_col.at[0], col_s.at[1], col_r.at[0], east),
    ]
    diagonal = [SW, SE, NW, NE]
    cors = []
    for i, d in enumerate(diagonal):
        dy, dx = DIRS[d]
        cors.append(
            remote(tx_cor.at[0 if dy < 0 else 1], rx_cor.at[3 - i], cor_s.at[i], cor_r.at[3 - i], device(dy, dx))
        )
    row2 = [
        remote(tx_row2.at[0], rx_row2.at[1], row2_s.at[0], row2_r.at[1], south),
        remote(tx_row2.at[1], rx_row2.at[0], row2_s.at[1], row2_r.at[0], north),
    ]
    first = row1 + cols + cors
    for copy in first + row2:
        copy.start()

    def tell(step):
        for d in (-(RADIUS << step), RADIUS << step):
            pl.semaphore_signal(known.at[step], inc=1, device_id=device(d, 0), device_id_type=MESH)
        for dev in plane:
            pl.semaphore_signal(known.at[3 + step], inc=1, device_id=dev, device_id_type=MESH)

    def told_by(step):
        pl.semaphore_wait(known.at[step], 2)

    def told_bx(step):
        pl.semaphore_wait(known.at[3 + step], len(plane))

    tell(0)

    for star in stars:
        star[0:PITCH, :] = jnp.zeros((PITCH, COLS), F32)
        star[PADDED - PITCH : PADDED, :] = jnp.zeros((PITCH, COLS), F32)

    told_by(0)
    told_bx(0)
    tell(1)
    for copy in first:
        copy.wait_recv()

    dep = {
        S: keep_s * rx_row1[0, 4 * KL : 4 * KL + 8],
        N: keep_n * rx_row1[1, 4 * KL : 4 * KL + 8],
        W: rx_col[0, 6],
        E: rx_col[1, 6],
        SW: keep_s * rx_cor[0, 0:8],
        SE: keep_s * rx_cor[1, 0:8],
        NW: keep_n * rx_cor[2, 0:8],
        NE: keep_n * rx_cor[3, 0:8],
    }

    def patch(own, near):
        beside = jnp.where(lane8 < 64, near[E], near[W])
        below = jnp.where(sub8 < 4, near[N], near[S])
        across = jnp.where(
            sub8 < 4, jnp.where(lane8 < 64, near[NE], near[NW]), jnp.where(lane8 < 64, near[SE], near[SW])
        )
        return jnp.concatenate(
            [jnp.concatenate([own, beside], axis=1), jnp.concatenate([below, across], axis=1)], axis=0
        )

    depth = patch(depth_v[...], dep)
    depths = (depth, roll(depth, -1, 1), roll(depth, 1, 1), roll(depth, -1, 0), roll(depth, 1, 0))
    for i, d in enumerate(depths):
        depths_v[i] = d

    rows1 = {}
    for side, (keep, place) in enumerate([(keep_s, PITCH - 1), (keep_n, PITCH + ROWS)]):
        for f, at in ((0, 0), (1, 2), (2, 3)):
            value = keep * rx_row1[side, at * KL : (at + 1) * KL]
            pads[f][pl.ds(place, KL, stride=PITCH), :] = value
            rows1[side, f] = value

    odd = lane8 % 4 >= 2
    for i in range(6):
        q_ref[i] = jnp.where(odd, rx_col[1, i], rx_col[0, i])
    lane_corner = [
        keep * jnp.where(odd, rx_cor[2 * side + 1, 16:24], rx_cor[2 * side, 16:24])
        for side, keep in enumerate((keep_s, keep_n))
    ]
    level_corner = [
        keep * jnp.where(lane8 % 2 == 1, rx_cor[2 * side + 1, 8:16], rx_cor[2 * side, 8:16])
        for side, keep in enumerate((keep_s, keep_n))
    ]

    level_rows = lax.broadcasted_iota(jnp.int32, (KL, COLS), 0).astype(F32)

    def star_rows(fields, second):
        for side, (row, place) in enumerate([(2 * ROWS - 1, PITCH - 1), (ROWS, PITCH + ROWS)]):
            near = [depths_v[i, row : row + 1, 0:COLS] for i in range(5)]
            terms = star_terms(level_rows, near, rows1[side, 1], rows1[side, 2])
            for f in fields:
                cell = rows1[side, f]
                inner = edge_row(f, 0 if side == 0 else ROWS - 1)
                outer = second(side, f)
                edge = jnp.concatenate(
                    [roll(level_corner[side], COLS - 1 - 2 * (6 * f + g), 1) for g in range(6)], axis=0
                )
                e, w = east_west(cell, edge)
                n, s = (inner, outer) if side == 0 else (outer, inner)
                stars[f][pl.ds(place, KL, stride=PITCH), :] = star_value(terms, cell, (e, w, n, s))

    def star_cols(fields):
        near = [
            jnp.where(odd, depths_v[i, 0:8, COLS : COLS + 1], depths_v[i, 0:8, 2 * COLS - 1 : 2 * COLS]) for i in range(5)
        ]
        for half in range(2):
            level = (lane8 // 4 + 32 * half).astype(F32)
            terms = star_terms(level, near, q_ref[2 + half], q_ref[4 + half])
            for f in fields:
                i = 2 * f + half
                cell, own = q_ref[i], tx_col[i]
                e = jnp.where(odd, roll(cell, -1, 1), roll(own, -1, 1))
                w = jnp.where(odd, roll(own, 1, 1), roll(cell, 1, 1))
                n = jnp.where(sub8 == ROWS - 1, lane_corner[1][i : i + 1], roll(cell, -1, 0))
                s = jnp.where(sub8 == 0, lane_corner[0][i : i + 1], roll(cell, 1, 0))
                qs_ref[i] = star_value(terms, cell, (e, w, n, s))

    def near_own():
        return [depths_v[i, 0:8, 0:COLS] for i in range(5)]

    def chunk_rows(ref, c):
        return ref.at[pl.ds(pl.multiple_of(c * (PITCH * CHUNK), PITCH * CHUNK), PITCH * (CHUNK + 2)), :]

    def edge_of(ref, f, c, l):
        shift = lax.rem(2 * COLS - 2 - 32 * lax.rem(c, 4) - 4 * l, COLS)
        return roll(ref[2 * f + c // 4], shift, 1)

    def star_own(fields, unroll):
        def step(c, carry):
            near = near_own()
            views = [chunk_rows(pad, c) for pad in pads]
            outs = [chunk_rows(star, c) for star in stars]
            for l in range(CHUNK):
                base = PITCH * (l + 1)
                level = (c * CHUNK + l).astype(F32)
                terms = star_terms(
                    level, near, views[1][pl.ds(base, 8), :], views[2][pl.ds(base, 8), :]
                )
                for f in fields:
                    cell = views[f][pl.ds(base, 8), :]
                    e, w = east_west(cell, edge_of(q_ref, f, c, l))
                    n = views[f][pl.ds(base + 1, 8), :]
                    s = views[f][pl.ds(base - 1, 8), :]
                    outs[f][pl.ds(base, 8), :] = star_value(terms, cell, (e, w, n, s))
            return carry

        lax.fori_loop(0, KL // CHUNK, step, 0, unroll=unroll)

    def update_own(fields, unroll):
        def step(c, total):
            near = near_own()
            views = [chunk_rows(star, c) for star in stars]
            for l in range(CHUNK):
                base = PITCH * (l + 1)
                level = (c * CHUNK + l).astype(F32)
                smooth = [jnp.where(level < d, F32(STEP_SMOOTH), F32(0.0)) for d in near[1:]]
                up = jnp.where(level + F32(1.0) < near[0], F32(STEP_VERT), F32(0.0))
                down = jnp.where(level > F32(0.0), F32(STEP_VERT), F32(0.0))
                own = F32(1.0) - (((smooth[0] + smooth[1]) + (smooth[2] + smooth[3])) + (up + down))
                centre = level < near[0]
                for f in fields:
                    view = views[f]
                    cell = view[pl.ds(base, 8), :]
                    e, w = east_west(cell, edge_of(qs_ref, f, c, l))
                    n = view[pl.ds(base + 1, 8), :]
                    s = view[pl.ds(base - 1, 8), :]
                    above = view[pl.ds(base + PITCH, 8), :]
                    below = view[pl.ds(base - PITCH, 8), :]
                    value = own * cell + F32(STEP_SMOOTH) * ((e + w) + (n + s)) + F32(STEP_VERT) * (above + below)
                    value = jnp.where(centre, value, F32(0.0))
                    fresh[f][c * CHUNK + l] = value
                    if f == 0:
                        total = total + value
            return total

        return lax.fori_loop(0, KL // CHUNK, step, jnp.zeros((8, COLS), F32), unroll=unroll)

    star_rows([0], lambda side, f: (keep_s, keep_n)[side] * rx_row1[side, KL : 2 * KL])
    star_cols([0])
    star_own([0], True)
    rhs = update_own([0], True) * F32(1.0 / math.sqrt(KL))

    height = depths_v[0] * F32(1.0 / KL)
    w_e = jnp.minimum(height, roll(height, -1, 1))
    w_n = jnp.minimum(height, roll(height, -1, 0))
    w_w = roll(w_e, 1, 1)
    w_s = roll(w_n, 1, 0)
    diag = F32(SURFACE_TERM) + w_e + w_w + w_n + w_s
    inverse = F32(1.0) / diag
    scaled = (w_e * inverse, w_w * inverse, w_n * inverse, w_s * inverse)

    tx_u[...] = rhs * inverse[0:8, 0:COLS]
    round_u = [
        remote(tx_u, rx_u.at[7 - i], u_s.at[i], u_r.at[7 - i], device(dy, dx)) for i, (dy, dx) in enumerate(DIRS)
    ]
    for copy in round_u:
        copy.start()
    told_by(1)
    told_bx(1)
    tell(2)
    for copy in round_u:
        copy.wait_recv()

    power = patch(tx_u[...], {d: rx_u[d] for d in range(8)})
    largest = jnp.max(jnp.max(jnp.abs(power), axis=0, keepdims=True), axis=1, keepdims=True)
    powers = [power]
    for _ in range(ITERS):
        e, w = roll(power, -1, 1), roll(power, 1, 1)
        n, s = roll(power, -1, 0), roll(power, 1, 0)
        power = (scaled[0] * e + scaled[1] * w) + (scaled[2] * n + scaled[3] * s)
        powers.append(power)
    own_diag = diag[0:8, 0:COLS]
    powers = [p[0:8, 0:COLS] for p in powers]
    steps = [powers[i] - powers[i + 1] for i in range(ITERS)]

    count = len(GRAM)
    grid = F32(4096.0 * 4.5) * largest * largest
    finer = grid * F32(1.0 / 4096.0)
    levels = ([], [], [])
    for i, j in GRAM:
        head, tail = two_prod(powers[i], powers[j])
        wide, extra = two_prod(own_diag, head)
        extra = extra + own_diag * tail
        coarse = (wide + grid) - grid
        wide = wide - coarse
        fine = (wide + finer) - finer
        for held, part in zip(levels, (coarse, fine, (wide - fine) + extra)):
            held.append(part)
    tiles = levels[0] + levels[1] + levels[2]
    tiles += [jnp.zeros((8, COLS), F32)] * (-len(tiles) % 8)
    row = jnp.zeros((8, COLS), F32)
    for c, tile in enumerate(sum_rows(tiles)):
        row = row + jnp.where(lane8 == sub8 + 8 * c, jnp.sum(tile, axis=1, keepdims=True), F32(0.0))
    row = jnp.sum(row, axis=0, keepdims=True)
    lane1 = lanes_of((1, COLS))
    last = jnp.logical_and(lane1 >= 2 * count, lane1 < 3 * count)

    tx_bx[...] = row
    told_bx(2)
    over_bx = [
        remote(tx_bx, rx_bx.at[o - 1], bx_s, bx_r, device(0, o)) for o in range(1, nbx)
    ]
    for copy in over_bx:
        copy.start()
    remote(rx_bx, rx_bx, bx_s, bx_r, east).wait_recv()
    row, lost = add_exact([row] + [rx_bx[i] for i in range(nbx - 1)])
    row = row + jnp.where(last, roll(lost, 2 * count, 1) + roll(lost, count, 1), F32(0.0))

    told_by(2)
    tx_by[...] = row
    rx_by[0:1, :] = row
    order = sorted(range(1, nby), key=lambda o: -min(o, nby - o))
    over_by = [remote(tx_by, rx_by.at[pl.ds(o, 1), :], by_s, by_r, device(o, 0)) for o in order]
    for copy in over_by:
        copy.start()

    for copy in row2:
        copy.wait_recv()
    star_rows([1, 2], lambda side, f: (keep_s, keep_n)[side] * rx_row2[side, (f - 1) * KL : f * KL])
    star_cols([1, 2])
    star_own([1, 2], 1)
    update_own([1, 2], 1)
    for copy in first + row2 + round_u:
        copy.wait_send()
    remote(rx_bx, rx_bx, bx_s, bx_r, east).wait_send()

    others = rx_by.at[pl.ds(1, nby - 1), :]
    remote(others, others, by_s, by_r, north).wait_recv()
    row, lost = add_exact([rx_by[i : i + 8] for i in range(0, nby, 8)])
    for shift in (4, 2, 1):
        row, more = two_sum(row, roll(row, shift, 0))
        lost = (lost + roll(lost, shift, 0)) + more
    row, lost = row[0:1], lost[0:1]
    head, tail = two_sum(row, roll(row, -count, 1))
    total = quick_sum(head, tail + ((roll(row, -2 * count, 1) + lost) + roll(lost, -count, 1)))

    gram = {}
    for k, (i, j) in enumerate(GRAM):
        gram[i, j] = gram[j, i] = tuple(part[0:1, k : k + 1] for part in total)
    system = [[sub2(gram[i, j], gram[i, j + 1]) for j in range(ITERS)] + [gram[i, 0]] for i in range(ITERS)]
    top = system[0]
    over = F32(1.0) / top[0][0]
    lower = []
    for i in (1, 2):
        ratio = system[i][0][0] * over
        left = []
        for j in range(ITERS + 1):
            head, tail = two_prod(ratio, top[j][0])
            value, lost = two_sum(system[i][j][0], -head)
            left.append((value, lost + (system[i][j][1] - (tail + ratio * top[j][1]))))
        ratio = (left[0][0] + left[0][1]) * over
        lower.append([quick_sum(left[j][0], left[j][1] - ratio * top[j][0]) for j in range(1, ITERS + 1)])
    (a11, a12, b1), (a21, a22, b2) = lower
    det = F32(1.0) / minor(a11, a22, a12, a21)
    c1 = minor(b1, a22, b2, a12) * det
    c2 = minor(b2, a11, b1, a21) * det
    c0 = ((top[3][0] - top[1][0] * c1) - top[2][0] * c2) * over

    surface = (c0 * powers[0] + c1 * powers[1]) + c2 * powers[2]
    resid = own_diag * (((powers[0] - c0 * steps[0]) - c1 * steps[1]) - c2 * steps[2])
    surface_out[...] = surface
    resid_out[...] = resid
    remote(others, others, by_s, by_r, north).wait_send()


def store(*refs):
    sources, targets, sems = refs[:5], refs[5:10], refs[10]
    copies = [pltpu.make_async_copy(src, dst, sems.at[i]) for i, (src, dst) in enumerate(zip(sources, targets))]
    for copy in copies:
        copy.start()
    for copy in copies:
        copy.wait()


def solution(mesh):
    nby, nbx = mesh.shape["by"], mesh.shape["bx"]

    def on_device(temp, uvel, vvel, kmt):
        field = jax.ShapeDtypeStruct(temp.shape, F32)
        plane = jax.ShapeDtypeStruct(kmt.shape, F32)
        vmem, dma = pltpu.VMEM, pltpu.SemaphoreType.DMA
        results = pl.pallas_call(
            lambda *refs: kernel(nby, nbx, *refs),
            out_shape=(*[pltpu.VMEM(temp.shape, F32)] * 3, *[pltpu.VMEM(kmt.shape, F32)] * 2),
            in_specs=[pl.BlockSpec(memory_space=pltpu.HBM)] * 4,
            out_specs=(pl.BlockSpec(memory_space=pltpu.VMEM),) * 5,
            scratch_shapes=[
                vmem((3, KL, ROWS, COLS), F32),
                vmem((ROWS, COLS), jnp.int32),
                *[vmem((PADDED, COLS), F32)] * 6,
                vmem((ROWS, COLS), F32),
                vmem((5, 2 * ROWS, 2 * COLS), F32),
                vmem((6, ROWS, COLS), F32),
                vmem((6, ROWS, COLS), F32),
                vmem((2, 4 * KL + 8, COLS), F32),
                vmem((2, 2 * KL, COLS), F32),
                vmem((7, ROWS, COLS), F32),
                vmem((2, 24, COLS), F32),
                vmem((2, 4 * KL + 8, COLS), F32),
                vmem((2, 2 * KL, COLS), F32),
                vmem((2, 7, ROWS, COLS), F32),
                vmem((4, 24, COLS), F32),
                vmem((ROWS, COLS), F32),
                vmem((8, ROWS, COLS), F32),
                vmem((1, COLS), F32),
                vmem((nbx - 1, 1, COLS), F32),
                vmem((1, COLS), F32),
                vmem((nby, COLS), F32),
                dma((4,)),
                dma((2,)), dma((2,)), dma((2,)), dma((2,)),
                dma((2,)), dma((2,)), dma((4,)), dma((4,)),
                dma((8,)), dma((8,)),
                dma, dma, dma, dma,
                pltpu.SemaphoreType.REGULAR((6,)),
            ],
            compiler_params=pltpu.CompilerParams(
                collective_id=0, has_side_effects=True, vmem_limit_bytes=32 * 1024 * 1024
            ),
        )(*[pltpu.with_memory_space_constraint(a, pltpu.HBM) for a in (temp, uvel, vvel, kmt)])
        return pl.pallas_call(
            store,
            out_shape=(field, field, field, plane, plane),
            in_specs=[pl.BlockSpec(memory_space=pltpu.VMEM)] * 5,
            out_specs=(pl.BlockSpec(memory_space=pltpu.HBM),) * 5,
            scratch_shapes=[dma((5,))],
            name="store",
        )(*[pltpu.with_memory_space_constraint(r, pltpu.VMEM) for r in results])

    in_specs = (P(None, "by", "bx"), P(None, "by", "bx"), P(None, "by", "bx"), P("by", "bx"))
    out_specs = (
        P(None, "by", "bx"),
        P(None, "by", "bx"),
        P(None, "by", "bx"),
        P("by", "bx"),
        P("by", "bx"),
    )
    return jax.shard_map(on_device, mesh=mesh, in_specs=in_specs, out_specs=out_specs, check_vma=False)
```

```python
import math

import jax
import jax.numpy as jnp
from jax import lax
from jax.experimental import pallas as pl
from jax.experimental.pallas import tpu as pltpu
from jax.sharding import PartitionSpec as P

ITERS = 3
STEP_DIFF = 0.1
STEP_ADV = 0.5
STEP_SMOOTH = 0.1
STEP_VERT = 0.2
SURFACE_TERM = 0.25

KL, ROWS, COLS = 48, 8, 128
CHUNK = 8
PITCH = 16
PADDED = PITCH * (KL + 2)
RADIUS = 4
WIDTH = 4

F32 = jnp.float32
MESH = pl.DeviceIdType.MESH

DIRS = [(-1, -1), (-1, 0), (-1, 1), (0, -1), (0, 1), (1, -1), (1, 0), (1, 1)]
SW, S, SE, W, E, NW, N, NE = range(8)

GRAM = [(i, j) for i in range(ITERS + 1) for j in range(i, ITERS + 1)]


def roll(value, shift, axis):
    size = value.shape[axis]
    return pltpu.roll(value, shift % size if isinstance(shift, int) else shift, axis)


def lanes_of(shape):
    return lax.broadcasted_iota(jnp.int32, shape, len(shape) - 1)


def east_west(value, edge):
    lane = lanes_of(value.shape)
    axis = value.ndim - 1
    east = roll(jnp.where(lane == 0, edge, value), -1, axis)
    west = roll(jnp.where(lane == COLS - 1, edge, value), 1, axis)
    return east, west


def star_terms(level, depths, uvel, vvel):
    centre = level < depths[0]
    diff = [jnp.where(level < d, F32(STEP_DIFF), F32(0.0)) for d in depths[1:]]
    own = F32(1.0) - ((diff[0] + diff[1]) + (diff[2] + diff[3]))
    adv_u = F32(0.5 * STEP_ADV) * uvel
    adv_v = F32(0.5 * STEP_ADV) * vvel
    return centre, own, (diff[0] - adv_u, diff[1] + adv_u, diff[2] - adv_v, diff[3] + adv_v)


def star_value(terms, cell, sides):
    centre, own, factors = terms
    total = own * cell
    for factor, side in zip(factors, sides):
        total = total + factor * side
    return jnp.where(centre, total, F32(0.0))


def two_sum(a, b):
    head = a + b
    shift = head - a
    return head, (a - (head - shift)) + (b - shift)


def quick_sum(a, b):
    head = a + b
    return head, b - (head - a)


def halves(a):
    wide = a * F32(4097.0)
    head = wide - (wide - a)
    return head, a - head


def two_prod(a, b):
    head = a * b
    (ah, al), (bh, bl) = halves(a), halves(b)
    return head, ((ah * bh - head) + ah * bl + al * bh) + al * bl


def add2(a, b):
    head, tail = two_sum(a[0], b[0])
    return quick_sum(head, tail + (a[1] + b[1]))


def sub2(a, b):
    return add2(a, (-b[0], -b[1]))


def minor(a, b, c, d):
    one, one_tail = two_prod(a[0], b[0])
    two, two_tail = two_prod(c[0], d[0])
    value, lost = two_sum(one, -two)
    one_tail = one_tail + (a[0] * b[1] + a[1] * b[0])
    return value + (lost + (one_tail - (two_tail + (c[0] * d[1] + c[1] * d[0]))))


def sum_rows(tiles):
    sub = lax.broadcasted_iota(jnp.int32, (8, COLS), 0)
    for shift in (1, 2, 4):
        mine = sub % (2 * shift) < shift
        tiles = [
            jnp.where(mine, one, other) + roll(jnp.where(mine, other, one), shift, 0)
            for one, other in zip(tiles[0::2], tiles[1::2])
        ]
    return tiles


def add_exact(rows):
    terms = [(row, None) for row in rows]
    while len(terms) > 1:
        paired = []
        for (a, lost_a), (b, lost_b) in zip(terms[0::2], terms[1::2]):
            head, lost = two_sum(a, b)
            for more in (lost_a, lost_b):
                lost = lost if more is None else lost + more
            paired.append((head, lost))
        terms = paired + ([terms[-1]] if len(terms) % 2 else [])
    total, lost = terms[0]
    return total, jnp.zeros_like(total) if lost is None else lost


def kernel(
    nby, nbx,
    temp_in, uvel_in, vvel_in, kmt_in,
    temp_out, uvel_out, vvel_out, surface_out, resid_out,
    raw, kmt_v, pad_t, pad_u, pad_v, star_t, star_u, star_v, depth_v, depths_v, q_ref, qs_ref, own_ref, beyond_ref,
    tx_row1, tx_row2, tx_col, tx_cor, rx_row1, rx_row2, rx_col, rx_cor,
    tx_u, rx_u, tx_bx, rx_bx, tx_by, rx_by,
    in_sem, row1_s, row1_r, row2_s, row2_r, col_s, col_r, cor_s, cor_r, u_s, u_r, bx_s, bx_r, by_s, by_r,
    known,
):
    by, bx = lax.axis_index("by"), lax.axis_index("bx")
    pads = (pad_t, pad_u, pad_v)
    stars = (star_t, star_u, star_v)
    fresh = (temp_out, uvel_out, vvel_out)

    def device(dy, dx):
        return (lax.rem(by + dy + nby, nby), lax.rem(bx + dx + nbx, nbx))

    loads = [
        pltpu.make_async_copy(src, dst, in_sem.at[i])
        for i, (src, dst) in enumerate(
            [(kmt_in, kmt_v), (temp_in, raw.at[0]), (uvel_in, raw.at[1]), (vvel_in, raw.at[2])]
        )
    ]
    for load in loads:
        load.start()

    barrier = pltpu.get_barrier_semaphore()
    across = lax.rem(bx, WIDTH)
    line = bx - across
    plane = [
        (by, line + lax.rem(across + 1, WIDTH)),
        (by, line + lax.rem(across + WIDTH - 1, WIDTH)),
        device(0, WIDTH),
        device(0, -WIDTH),
    ]
    greeted = [device(dy, dx) for dy, dx in DIRS if dx]
    greeted += [device(d, 0) for d in range(-RADIUS, RADIUS + 1) if d]
    greeted += plane
    for dev in greeted:
        pl.semaphore_signal(barrier, inc=1, device_id=dev, device_id_type=MESH)

    keep_s = jnp.where(by == 0, F32(0.0), F32(1.0))
    keep_n = jnp.where(by == nby - 1, F32(0.0), F32(1.0))
    lane8 = lanes_of((8, COLS))
    sub8 = lax.broadcasted_iota(jnp.int32, (8, COLS), 0)

    loads[0].wait()
    depth_v[...] = kmt_v[...].astype(F32)
    for f in range(3):
        loads[1 + f].wait()
        pad = pads[f]

        quads = []
        for c in range(KL // CHUNK):
            packed = jnp.zeros((8, COLS), F32)
            for l in range(CHUNK):
                k = c * CHUNK + l
                tile = raw[f, k]
                pad[PITCH * (k + 1) : PITCH * (k + 1) + 8, :] = tile
                packed = jnp.where(lane8 // 4 == k % 32, roll(tile, 2 + 4 * (k % 32), 1), packed)
            quads.append(packed)
        tx_col[2 * f] = (quads[0] + quads[1]) + (quads[2] + quads[3])
        tx_col[2 * f + 1] = quads[4] + quads[5]
    tx_col[6] = depth_v[...]

    def edge_row(f, row):
        return pads[f][pl.ds(PITCH + row, KL, stride=PITCH), :]

    lane_row = lanes_of((8, COLS))
    for side, (row, inner) in enumerate([(0, 1), (ROWS - 1, ROWS - 2)]):
        edges = [edge_row(f, row) for f in range(3)]
        tx_row1[side, 0:KL] = edges[0]
        tx_row1[side, KL : 2 * KL] = edge_row(0, inner)
        tx_row1[side, 2 * KL : 3 * KL] = edges[1]
        tx_row1[side, 3 * KL : 4 * KL] = edges[2]
        tx_row1[side, 4 * KL : 4 * KL + 8] = depth_v[...]
        tx_row2[side, 0:KL] = edge_row(1, inner)
        tx_row2[side, KL : 2 * KL] = edge_row(2, inner)
        corner = jnp.zeros((8, COLS), F32)
        for f in range(3):
            for g in range(6):
                at = 2 * (6 * f + g)
                corner = jnp.where(lane_row // 2 == at // 2, roll(edges[f][8 * g : 8 * g + 8], 1 + at, 1), corner)
        tx_cor[side, 0:8] = depth_v[...]
        tx_cor[side, 8:16] = corner
        for i in range(6):
            tx_cor[side, 16 + i : 17 + i] = tx_col[i, row : row + 1]
        tx_cor[side, 22:24] = jnp.zeros((2, COLS), F32)

    def remote(src, dst, send, recv, dev):
        return pltpu.make_async_remote_copy(
            src_ref=src, dst_ref=dst, send_sem=send, recv_sem=recv, device_id=dev, device_id_type=MESH
        )

    pl.semaphore_wait(barrier, len(greeted))

    south, north, west, east = device(-1, 0), device(1, 0), device(0, -1), device(0, 1)
    row1 = [
        remote(tx_row1.at[0], rx_row1.at[1], row1_s.at[0], row1_r.at[1], south),
        remote(tx_row1.at[1], rx_row1.at[0], row1_s.at[1], row1_r.at[0], north),
    ]
    cols = [
        remote(tx_col, rx_col.at[1], col_s.at[0], col_r.at[1], west),
        remote(tx_col, rx_col.at[0], col_s.at[1], col_r.at[0], east),
    ]
    diagonal = [SW, SE, NW, NE]
    cors = []
    for i, d in enumerate(diagonal):
        dy, dx = DIRS[d]
        cors.append(
            remote(tx_cor.at[0 if dy < 0 else 1], rx_cor.at[3 - i], cor_s.at[i], cor_r.at[3 - i], device(dy, dx))
        )
    row2 = [
        remote(tx_row2.at[0], rx_row2.at[1], row2_s.at[0], row2_r.at[1], south),
        remote(tx_row2.at[1], rx_row2.at[0], row2_s.at[1], row2_r.at[0], north),
    ]
    first = row1 + cols + cors
    for copy in first + row2:
        copy.start()

    def tell(step):
        for d in (-(RADIUS << step), RADIUS << step):
            pl.semaphore_signal(known.at[step], inc=1, device_id=device(d, 0), device_id_type=MESH)
        for dev in plane:
            pl.semaphore_signal(known.at[3 + step], inc=1, device_id=dev, device_id_type=MESH)

    def told_by(step):
        pl.semaphore_wait(known.at[step], 2)

    def told_bx(step):
        pl.semaphore_wait(known.at[3 + step], len(plane))

    tell(0)

    for star in stars:
        star[0:PITCH, :] = jnp.zeros((PITCH, COLS), F32)
        star[PADDED - PITCH : PADDED, :] = jnp.zeros((PITCH, COLS), F32)

    def chunk_rows(ref, c):
        return ref.at[pl.ds(pl.multiple_of(c * (PITCH * CHUNK), PITCH * CHUNK), PITCH * (CHUNK + 2)), :]

    inside = [
        depth_v[...],
        jnp.where(lane8 == COLS - 1, F32(0.0), roll(depth_v[...], -1, 1)),
        jnp.where(lane8 == 0, F32(0.0), roll(depth_v[...], 1, 1)),
        jnp.where(sub8 == ROWS - 1, F32(0.0), roll(depth_v[...], -1, 0)),
        jnp.where(sub8 == 0, F32(0.0), roll(depth_v[...], 1, 0)),
    ]

    def star_inside(c, carry):
        views = [chunk_rows(pad, c) for pad in pads]
        out = chunk_rows(star_t, c)
        for l in range(CHUNK):
            base = PITCH * (l + 1)
            level = (c * CHUNK + l).astype(F32)
            terms = star_terms(level, inside, views[1][pl.ds(base, 8), :], views[2][pl.ds(base, 8), :])
            cell = views[0][pl.ds(base, 8), :]
            e = jnp.where(lane8 == COLS - 1, F32(0.0), roll(cell, -1, 1))
            w = jnp.where(lane8 == 0, F32(0.0), roll(cell, 1, 1))
            n = jnp.where(sub8 == ROWS - 1, F32(0.0), roll(cell, -1, 0))
            s = jnp.where(sub8 == 0, F32(0.0), roll(cell, 1, 0))
            out[pl.ds(base, 8), :] = star_value(terms, cell, (e, w, n, s))
            smooth = [jnp.where(level < d, F32(STEP_SMOOTH), F32(0.0)) for d in inside[1:]]
            up = jnp.where(level + F32(1.0) < inside[0], F32(STEP_VERT), F32(0.0))
            down = jnp.where(level > F32(0.0), F32(STEP_VERT), F32(0.0))
            own_ref[c * CHUNK + l] = F32(1.0) - (((smooth[0] + smooth[1]) + (smooth[2] + smooth[3])) + (up + down))
        return carry

    lax.fori_loop(0, KL // CHUNK, star_inside, 0)

    told_by(0)
    told_bx(0)
    tell(1)
    for copy in first:
        copy.wait_recv()

    dep = {
        S: keep_s * rx_row1[0, 4 * KL : 4 * KL + 8],
        N: keep_n * rx_row1[1, 4 * KL : 4 * KL + 8],
        W: rx_col[0, 6],
        E: rx_col[1, 6],
        SW: keep_s * rx_cor[0, 0:8],
        SE: keep_s * rx_cor[1, 0:8],
        NW: keep_n * rx_cor[2, 0:8],
        NE: keep_n * rx_cor[3, 0:8],
    }

    def patch(own, near):
        beside = jnp.where(lane8 < 64, near[E], near[W])
        below = jnp.where(sub8 < 4, near[N], near[S])
        across = jnp.where(
            sub8 < 4, jnp.where(lane8 < 64, near[NE], near[NW]), jnp.where(lane8 < 64, near[SE], near[SW])
        )
        return jnp.concatenate(
            [jnp.concatenate([own, beside], axis=1), jnp.concatenate([below, across], axis=1)], axis=0
        )

    depth = patch(depth_v[...], dep)
    depths = (depth, roll(depth, -1, 1), roll(depth, 1, 1), roll(depth, -1, 0), roll(depth, 1, 0))
    for i, d in enumerate(depths):
        depths_v[i] = d

    rows1 = {}
    for side, (keep, place) in enumerate([(keep_s, PITCH - 1), (keep_n, PITCH + ROWS)]):
        for f, at in ((0, 0), (1, 2), (2, 3)):
            value = keep * rx_row1[side, at * KL : (at + 1) * KL]
            pads[f][pl.ds(place, KL, stride=PITCH), :] = value
            rows1[side, f] = value

    odd = lane8 % 4 >= 2
    for i in range(6):
        q_ref[i] = jnp.where(odd, rx_col[1, i], rx_col[0, i])
    lane_corner = [
        keep * jnp.where(odd, rx_cor[2 * side + 1, 16:24], rx_cor[2 * side, 16:24])
        for side, keep in enumerate((keep_s, keep_n))
    ]
    level_corner = [
        keep * jnp.where(lane8 % 2 == 1, rx_cor[2 * side + 1, 8:16], rx_cor[2 * side, 8:16])
        for side, keep in enumerate((keep_s, keep_n))
    ]

    level_rows = lax.broadcasted_iota(jnp.int32, (KL, COLS), 0).astype(F32)

    def star_rows(fields, second):
        for side, (row, place) in enumerate([(2 * ROWS - 1, PITCH - 1), (ROWS, PITCH + ROWS)]):
            near = [depths_v[i, row : row + 1, 0:COLS] for i in range(5)]
            terms = star_terms(level_rows, near, rows1[side, 1], rows1[side, 2])
            for f in fields:
                cell = rows1[side, f]
                inner = edge_row(f, 0 if side == 0 else ROWS - 1)
                outer = second(side, f)
                edge = jnp.concatenate(
                    [roll(level_corner[side], COLS - 1 - 2 * (6 * f + g), 1) for g in range(6)], axis=0
                )
                e, w = east_west(cell, edge)
                n, s = (inner, outer) if side == 0 else (outer, inner)
                stars[f][pl.ds(place, KL, stride=PITCH), :] = star_value(terms, cell, (e, w, n, s))

    def star_cols(fields):
        near = [
            jnp.where(odd, depths_v[i, 0:8, COLS : COLS + 1], depths_v[i, 0:8, 2 * COLS - 1 : 2 * COLS]) for i in range(5)
        ]
        for half in range(2):
            level = (lane8 // 4 + 32 * half).astype(F32)
            terms = star_terms(level, near, q_ref[2 + half], q_ref[4 + half])
            for f in fields:
                i = 2 * f + half
                cell, own = q_ref[i], tx_col[i]
                e = jnp.where(odd, roll(cell, -1, 1), roll(own, -1, 1))
                w = jnp.where(odd, roll(own, 1, 1), roll(cell, 1, 1))
                n = jnp.where(sub8 == ROWS - 1, lane_corner[1][i : i + 1], roll(cell, -1, 0))
                s = jnp.where(sub8 == 0, lane_corner[0][i : i + 1], roll(cell, 1, 0))
                qs_ref[i] = star_value(terms, cell, (e, w, n, s))

    def near_own():
        return [depths_v[i, 0:8, 0:COLS] for i in range(5)]

    def edge_of(ref, f, c, l):
        shift = lax.rem(2 * COLS - 2 - 32 * lax.rem(c, 4) - 4 * l, COLS)
        return roll(ref[2 * f + c // 4], shift, 1)

    def star_own(fields, unroll):
        def step(c, carry):
            near = near_own()
            views = [chunk_rows(pad, c) for pad in pads]
            outs = [chunk_rows(star, c) for star in stars]
            for l in range(CHUNK):
                base = PITCH * (l + 1)
                level = (c * CHUNK + l).astype(F32)
                terms = star_terms(
                    level, near, views[1][pl.ds(base, 8), :], views[2][pl.ds(base, 8), :]
                )
                for f in fields:
                    cell = views[f][pl.ds(base, 8), :]
                    e, w = east_west(cell, edge_of(q_ref, f, c, l))
                    n = views[f][pl.ds(base + 1, 8), :]
                    s = views[f][pl.ds(base - 1, 8), :]
                    outs[f][pl.ds(base, 8), :] = star_value(terms, cell, (e, w, n, s))
            return carry

        lax.fori_loop(0, KL // CHUNK, step, 0, unroll=unroll)

    def update_own(fields, unroll):
        def step(c, total):
            near = near_own()
            views = [chunk_rows(star, c) for star in stars]
            for l in range(CHUNK):
                base = PITCH * (l + 1)
                level = (c * CHUNK + l).astype(F32)
                smooth = [jnp.where(level < d, F32(STEP_SMOOTH), F32(0.0)) for d in near[1:]]
                up = jnp.where(level + F32(1.0) < near[0], F32(STEP_VERT), F32(0.0))
                down = jnp.where(level > F32(0.0), F32(STEP_VERT), F32(0.0))
                own = F32(1.0) - (((smooth[0] + smooth[1]) + (smooth[2] + smooth[3])) + (up + down))
                centre = level < near[0]
                for f in fields:
                    view = views[f]
                    cell = view[pl.ds(base, 8), :]
                    e, w = east_west(cell, edge_of(qs_ref, f, c, l))
                    n = view[pl.ds(base + 1, 8), :]
                    s = view[pl.ds(base - 1, 8), :]
                    above = view[pl.ds(base + PITCH, 8), :]
                    below = view[pl.ds(base - PITCH, 8), :]
                    value = own * cell + F32(STEP_SMOOTH) * ((e + w) + (n + s)) + F32(STEP_VERT) * (above + below)
                    value = jnp.where(centre, value, F32(0.0))
                    fresh[f][c * CHUNK + l] = value
                    if f == 0:
                        total = total + value
            return total

        return lax.fori_loop(0, KL // CHUNK, step, jnp.zeros((8, COLS), F32), unroll=unroll)

    def add_beyond():
        for side, row in enumerate((0, ROWS - 1)):
            cell, halo = edge_row(0, row), rows1[side, 0]
            adv = F32(0.5 * STEP_ADV) * edge_row(2, row)
            centre = level_rows < depths_v[0, row : row + 1, 0:COLS]
            beyond = level_rows < depths_v[4 - side, row : row + 1, 0:COLS]
            more = jnp.where(beyond, F32(STEP_DIFF) * (halo - cell), F32(0.0))
            more = more + adv * halo if side == 0 else more - adv * halo
            place = pl.ds(PITCH + row, KL, stride=PITCH)
            star_t[place, :] = star_t[place, :] + jnp.where(centre, more, F32(0.0))
        here = jnp.where(odd, depth_v[:, 0:1], depth_v[:, COLS - 1 : COLS])
        near = jnp.where(odd, depths_v[0, 0:8, 2 * COLS - 1 : 2 * COLS], depths_v[0, 0:8, COLS : COLS + 1])
        for half in range(2):
            level = (lane8 // 4 + 32 * half).astype(F32)
            cell = tx_col[half]
            halo = jnp.where(odd, roll(q_ref[half], 1, 1), roll(q_ref[half], -1, 1))
            adv = F32(0.5 * STEP_ADV) * tx_col[2 + half] * halo
            more = jnp.where(level < near, F32(STEP_DIFF) * (halo - cell), F32(0.0)) + jnp.where(odd, adv, -adv)
            beyond_ref[half] = jnp.where(level < here, more, F32(0.0))
        rim = jnp.logical_or(lane8 == 0, lane8 == COLS - 1)
        for k in range(KL):
            place = pl.ds(PITCH * (k + 1), 8)
            edge = roll(beyond_ref[k // 32], COLS - 2 - 4 * (k % 32), 1)
            star_t[place, :] = star_t[place, :] + jnp.where(rim, edge, F32(0.0))

    def update_tracer():
        rim_rows = jnp.where(sub8 == 0, depths_v[4, 0:8, 0:COLS], F32(0.0))
        rim_rows = jnp.where(sub8 == ROWS - 1, depths_v[3, 0:8, 0:COLS], rim_rows)
        rim_lanes = jnp.where(lane8 == 0, depths_v[2, 0:8, 0:COLS], F32(0.0))
        rim_lanes = jnp.where(lane8 == COLS - 1, depths_v[1, 0:8, 0:COLS], rim_lanes)
        depth_own = depth_v[...]
        total = [jnp.zeros((8, COLS), F32)] * 4
        for k in range(KL):
            base = PITCH * (k + 1)
            cell = star_t[pl.ds(base, 8), :]
            e, w = east_west(cell, roll(qs_ref[k // 32], COLS - 2 - 4 * (k % 32), 1))
            n = star_t[pl.ds(base + 1, 8), :]
            s = star_t[pl.ds(base - 1, 8), :]
            above = star_t[pl.ds(base + PITCH, 8), :]
            below = star_t[pl.ds(base - PITCH, 8), :]
            own = own_ref[k] - jnp.where(rim_rows > F32(k), F32(STEP_SMOOTH), F32(0.0))
            own = own - jnp.where(rim_lanes > F32(k), F32(STEP_SMOOTH), F32(0.0))
            value = own * cell + F32(STEP_SMOOTH) * ((e + w) + (n + s)) + F32(STEP_VERT) * (above + below)
            value = jnp.where(depth_own > F32(k), value, F32(0.0))
            temp_out[k] = value
            total[k % 4] = total[k % 4] + value
        return (total[0] + total[1]) + (total[2] + total[3])

    add_beyond()
    star_rows([0], lambda side, f: (keep_s, keep_n)[side] * rx_row1[side, KL : 2 * KL])
    star_cols([0])
    rhs = update_tracer() * F32(1.0 / math.sqrt(KL))

    height = depths_v[0] * F32(1.0 / KL)
    w_e = jnp.minimum(height, roll(height, -1, 1))
    w_n = jnp.minimum(height, roll(height, -1, 0))
    w_w = roll(w_e, 1, 1)
    w_s = roll(w_n, 1, 0)
    diag = F32(SURFACE_TERM) + w_e + w_w + w_n + w_s
    inverse = F32(1.0) / diag
    scaled = (w_e * inverse, w_w * inverse, w_n * inverse, w_s * inverse)

    tx_u[...] = rhs * inverse[0:8, 0:COLS]
    round_u = [
        remote(tx_u, rx_u.at[7 - i], u_s.at[i], u_r.at[7 - i], device(dy, dx)) for i, (dy, dx) in enumerate(DIRS)
    ]
    for copy in round_u:
        copy.start()
    told_by(1)
    told_bx(1)
    tell(2)
    for copy in round_u:
        copy.wait_recv()

    power = patch(tx_u[...], {d: rx_u[d] for d in range(8)})
    largest = jnp.max(jnp.max(jnp.abs(power), axis=0, keepdims=True), axis=1, keepdims=True)
    powers = [power]
    for _ in range(ITERS):
        e, w = roll(power, -1, 1), roll(power, 1, 1)
        n, s = roll(power, -1, 0), roll(power, 1, 0)
        power = (scaled[0] * e + scaled[1] * w) + (scaled[2] * n + scaled[3] * s)
        powers.append(power)
    own_diag = diag[0:8, 0:COLS]
    powers = [p[0:8, 0:COLS] for p in powers]
    steps = [powers[i] - powers[i + 1] for i in range(ITERS)]

    count = len(GRAM)
    grid = F32(4096.0 * 4.5) * largest * largest
    finer = grid * F32(1.0 / 4096.0)
    levels = ([], [], [])
    for i, j in GRAM:
        head, tail = two_prod(powers[i], powers[j])
        wide, extra = two_prod(own_diag, head)
        extra = extra + own_diag * tail
        coarse = (wide + grid) - grid
        wide = wide - coarse
        fine = (wide + finer) - finer
        for held, part in zip(levels, (coarse, fine, (wide - fine) + extra)):
            held.append(part)
    tiles = levels[0] + levels[1] + levels[2]
    tiles += [jnp.zeros((8, COLS), F32)] * (-len(tiles) % 8)
    row = jnp.zeros((8, COLS), F32)
    for c, tile in enumerate(sum_rows(tiles)):
        row = row + jnp.where(lane8 == sub8 + 8 * c, jnp.sum(tile, axis=1, keepdims=True), F32(0.0))
    row = jnp.sum(row, axis=0, keepdims=True)
    lane1 = lanes_of((1, COLS))
    last = jnp.logical_and(lane1 >= 2 * count, lane1 < 3 * count)

    tx_bx[...] = row
    told_bx(2)
    over_bx = [
        remote(tx_bx, rx_bx.at[o - 1], bx_s, bx_r, device(0, o)) for o in range(1, nbx)
    ]
    for copy in over_bx:
        copy.start()
    remote(rx_bx, rx_bx, bx_s, bx_r, east).wait_recv()
    row, lost = add_exact([row] + [rx_bx[i] for i in range(nbx - 1)])
    row = row + jnp.where(last, roll(lost, 2 * count, 1) + roll(lost, count, 1), F32(0.0))

    told_by(2)
    tx_by[...] = row
    rx_by[0:1, :] = row
    order = sorted(range(1, nby), key=lambda o: -min(o, nby - o))
    over_by = [remote(tx_by, rx_by.at[pl.ds(o, 1), :], by_s, by_r, device(o, 0)) for o in order]
    for copy in over_by:
        copy.start()

    for copy in row2:
        copy.wait_recv()
    star_rows([1, 2], lambda side, f: (keep_s, keep_n)[side] * rx_row2[side, (f - 1) * KL : f * KL])
    star_cols([1, 2])
    star_own([1, 2], 1)
    update_own([1, 2], 1)
    for copy in first + row2 + round_u:
        copy.wait_send()
    remote(rx_bx, rx_bx, bx_s, bx_r, east).wait_send()

    others = rx_by.at[pl.ds(1, nby - 1), :]
    remote(others, others, by_s, by_r, north).wait_recv()
    row, lost = add_exact([rx_by[i : i + 8] for i in range(0, nby, 8)])
    for shift in (4, 2, 1):
        row, more = two_sum(row, roll(row, shift, 0))
        lost = (lost + roll(lost, shift, 0)) + more
    row, lost = row[0:1], lost[0:1]
    head, tail = two_sum(row, roll(row, -count, 1))
    total = quick_sum(head, tail + ((roll(row, -2 * count, 1) + lost) + roll(lost, -count, 1)))

    gram = {}
    for k, (i, j) in enumerate(GRAM):
        gram[i, j] = gram[j, i] = tuple(part[0:1, k : k + 1] for part in total)
    system = [[sub2(gram[i, j], gram[i, j + 1]) for j in range(ITERS)] + [gram[i, 0]] for i in range(ITERS)]
    top = system[0]
    over = F32(1.0) / top[0][0]
    lower = []
    for i in (1, 2):
        ratio = system[i][0][0] * over
        left = []
        for j in range(ITERS + 1):
            head, tail = two_prod(ratio, top[j][0])
            value, lost = two_sum(system[i][j][0], -head)
            left.append((value, lost + (system[i][j][1] - (tail + ratio * top[j][1]))))
        ratio = (left[0][0] + left[0][1]) * over
        lower.append([quick_sum(left[j][0], left[j][1] - ratio * top[j][0]) for j in range(1, ITERS + 1)])
    (a11, a12, b1), (a21, a22, b2) = lower
    det = F32(1.0) / minor(a11, a22, a12, a21)
    c1 = minor(b1, a22, b2, a12) * det
    c2 = minor(b2, a11, b1, a21) * det
    c0 = ((top[3][0] - top[1][0] * c1) - top[2][0] * c2) * over

    surface = (c0 * powers[0] + c1 * powers[1]) + c2 * powers[2]
    resid = own_diag * (((powers[0] - c0 * steps[0]) - c1 * steps[1]) - c2 * steps[2])
    surface_out[...] = surface
    resid_out[...] = resid
    remote(others, others, by_s, by_r, north).wait_send()


def store(*refs):
    sources, targets, sems = refs[:5], refs[5:10], refs[10]
    copies = [pltpu.make_async_copy(src, dst, sems.at[i]) for i, (src, dst) in enumerate(zip(sources, targets))]
    for copy in copies:
        copy.start()
    for copy in copies:
        copy.wait()


def solution(mesh):
    nby, nbx = mesh.shape["by"], mesh.shape["bx"]

    def on_device(temp, uvel, vvel, kmt):
        field = jax.ShapeDtypeStruct(temp.shape, F32)
        plane = jax.ShapeDtypeStruct(kmt.shape, F32)
        vmem, dma = pltpu.VMEM, pltpu.SemaphoreType.DMA
        results = pl.pallas_call(
            lambda *refs: kernel(nby, nbx, *refs),
            out_shape=(*[pltpu.VMEM(temp.shape, F32)] * 3, *[pltpu.VMEM(kmt.shape, F32)] * 2),
            in_specs=[pl.BlockSpec(memory_space=pltpu.HBM)] * 4,
            out_specs=(pl.BlockSpec(memory_space=pltpu.VMEM),) * 5,
            scratch_shapes=[
                vmem((3, KL, ROWS, COLS), F32),
                vmem((ROWS, COLS), jnp.int32),
                *[vmem((PADDED, COLS), F32)] * 6,
                vmem((ROWS, COLS), F32),
                vmem((5, 2 * ROWS, 2 * COLS), F32),
                vmem((6, ROWS, COLS), F32),
                vmem((6, ROWS, COLS), F32),
                vmem((KL, ROWS, COLS), F32),
                vmem((2, ROWS, COLS), F32),
                vmem((2, 4 * KL + 8, COLS), F32),
                vmem((2, 2 * KL, COLS), F32),
                vmem((7, ROWS, COLS), F32),
                vmem((2, 24, COLS), F32),
                vmem((2, 4 * KL + 8, COLS), F32),
                vmem((2, 2 * KL, COLS), F32),
                vmem((2, 7, ROWS, COLS), F32),
                vmem((4, 24, COLS), F32),
                vmem((ROWS, COLS), F32),
                vmem((8, ROWS, COLS), F32),
                vmem((1, COLS), F32),
                vmem((nbx - 1, 1, COLS), F32),
                vmem((1, COLS), F32),
                vmem((nby, COLS), F32),
                dma((4,)),
                dma((2,)), dma((2,)), dma((2,)), dma((2,)),
                dma((2,)), dma((2,)), dma((4,)), dma((4,)),
                dma((8,)), dma((8,)),
                dma, dma, dma, dma,
                pltpu.SemaphoreType.REGULAR((6,)),
            ],
            compiler_params=pltpu.CompilerParams(
                collective_id=0, has_side_effects=True, vmem_limit_bytes=32 * 1024 * 1024
            ),
        )(*[pltpu.with_memory_space_constraint(a, pltpu.HBM) for a in (temp, uvel, vvel, kmt)])
        return pl.pallas_call(
            store,
            out_shape=(field, field, field, plane, plane),
            in_specs=[pl.BlockSpec(memory_space=pltpu.VMEM)] * 5,
            out_specs=(pl.BlockSpec(memory_space=pltpu.HBM),) * 5,
            scratch_shapes=[dma((5,))],
            name="store",
        )(*[pltpu.with_memory_space_constraint(r, pltpu.VMEM) for r in results])

    in_specs = (P(None, "by", "bx"), P(None, "by", "bx"), P(None, "by", "bx"), P("by", "bx"))
    out_specs = (
        P(None, "by", "bx"),
        P(None, "by", "bx"),
        P(None, "by", "bx"),
        P("by", "bx"),
        P("by", "bx"),
    )
    return jax.shard_map(on_device, mesh=mesh, in_specs=in_specs, out_specs=out_specs, check_vma=False)
```

```python
import math

import jax
import jax.numpy as jnp
from jax import lax
from jax.experimental import pallas as pl
from jax.experimental.pallas import tpu as pltpu
from jax.sharding import PartitionSpec as P

ITERS = 3
STEP_DIFF = 0.1
STEP_ADV = 0.5
STEP_SMOOTH = 0.1
STEP_VERT = 0.2
SURFACE_TERM = 0.25

KL, ROWS, COLS = 48, 8, 128
CHUNK = 8
PITCH = 16
PADDED = PITCH * (KL + 2)
RADIUS = 4
WIDTH = 4

F32 = jnp.float32
MESH = pl.DeviceIdType.MESH

DIRS = [(-1, -1), (-1, 0), (-1, 1), (0, -1), (0, 1), (1, -1), (1, 0), (1, 1)]
SW, S, SE, W, E, NW, N, NE = range(8)

GRAM = [(i, j) for i in range(ITERS + 1) for j in range(i, ITERS + 1)]


def roll(value, shift, axis):
    size = value.shape[axis]
    return pltpu.roll(value, shift % size if isinstance(shift, int) else shift, axis)


def lanes_of(shape):
    return lax.broadcasted_iota(jnp.int32, shape, len(shape) - 1)


def east_west(value, edge):
    lane = lanes_of(value.shape)
    axis = value.ndim - 1
    east = roll(jnp.where(lane == 0, edge, value), -1, axis)
    west = roll(jnp.where(lane == COLS - 1, edge, value), 1, axis)
    return east, west


def star_terms(level, depths, uvel, vvel):
    centre = level < depths[0]
    diff = [jnp.where(level < d, F32(STEP_DIFF), F32(0.0)) for d in depths[1:]]
    own = F32(1.0) - ((diff[0] + diff[1]) + (diff[2] + diff[3]))
    adv_u = F32(0.5 * STEP_ADV) * uvel
    adv_v = F32(0.5 * STEP_ADV) * vvel
    return centre, own, (diff[0] - adv_u, diff[1] + adv_u, diff[2] - adv_v, diff[3] + adv_v)


def star_value(terms, cell, sides):
    centre, own, factors = terms
    total = own * cell
    for factor, side in zip(factors, sides):
        total = total + factor * side
    return jnp.where(centre, total, F32(0.0))


def two_sum(a, b):
    head = a + b
    shift = head - a
    return head, (a - (head - shift)) + (b - shift)


def quick_sum(a, b):
    head = a + b
    return head, b - (head - a)


def halves(a):
    wide = a * F32(4097.0)
    head = wide - (wide - a)
    return head, a - head


def two_prod(a, b):
    head = a * b
    (ah, al), (bh, bl) = halves(a), halves(b)
    return head, ((ah * bh - head) + ah * bl + al * bh) + al * bl


def add2(a, b):
    head, tail = two_sum(a[0], b[0])
    return quick_sum(head, tail + (a[1] + b[1]))


def sub2(a, b):
    return add2(a, (-b[0], -b[1]))


def minor(a, b, c, d):
    one, one_tail = two_prod(a[0], b[0])
    two, two_tail = two_prod(c[0], d[0])
    value, lost = two_sum(one, -two)
    one_tail = one_tail + (a[0] * b[1] + a[1] * b[0])
    return value + (lost + (one_tail - (two_tail + (c[0] * d[1] + c[1] * d[0]))))


def sum_rows(tiles):
    sub = lax.broadcasted_iota(jnp.int32, (8, COLS), 0)
    for shift in (1, 2, 4):
        mine = sub % (2 * shift) < shift
        tiles = [
            jnp.where(mine, one, other) + roll(jnp.where(mine, other, one), shift, 0)
            for one, other in zip(tiles[0::2], tiles[1::2])
        ]
    return tiles


def add_exact(rows):
    terms = [(row, None) for row in rows]
    while len(terms) > 1:
        paired = []
        for (a, lost_a), (b, lost_b) in zip(terms[0::2], terms[1::2]):
            head, lost = two_sum(a, b)
            for more in (lost_a, lost_b):
                lost = lost if more is None else lost + more
            paired.append((head, lost))
        terms = paired + ([terms[-1]] if len(terms) % 2 else [])
    total, lost = terms[0]
    return total, jnp.zeros_like(total) if lost is None else lost


def kernel(
    nby, nbx,
    temp_in, uvel_in, vvel_in, kmt_in,
    temp_out, uvel_out, vvel_out, surface_out, resid_out,
    raw, kmt_v, pad_t, pad_u, pad_v, star_t, star_u, star_v, depth_v, depths_v, q_ref, qs_ref, own_ref, beyond_ref,
    tx_row1, tx_row2, tx_col, tx_cor, rx_row1, rx_row2, rx_col, rx_cor,
    tx_u, rx_u, tx_bx, rx_bx, tx_by, rx_by,
    in_sem, row1_s, row1_r, row2_s, row2_r, col_s, col_r, cor_s, cor_r, u_s, u_r, bx_s, bx_r, by_s, by_r,
    known,
):
    by, bx = lax.axis_index("by"), lax.axis_index("bx")
    pads = (pad_t, pad_u, pad_v)
    stars = (star_t, star_u, star_v)
    fresh = (temp_out, uvel_out, vvel_out)

    def device(dy, dx):
        return (lax.rem(by + dy + nby, nby), lax.rem(bx + dx + nbx, nbx))

    loads = [
        pltpu.make_async_copy(src, dst, in_sem.at[i])
        for i, (src, dst) in enumerate(
            [(kmt_in, kmt_v), (temp_in, raw.at[0]), (uvel_in, raw.at[1]), (vvel_in, raw.at[2])]
        )
    ]
    for load in loads:
        load.start()

    barrier = pltpu.get_barrier_semaphore()
    across = lax.rem(bx, WIDTH)
    line = bx - across
    plane = [
        (by, line + lax.rem(across + 1, WIDTH)),
        (by, line + lax.rem(across + WIDTH - 1, WIDTH)),
        device(0, WIDTH),
        device(0, -WIDTH),
    ]
    greeted = [device(dy, dx) for dy, dx in DIRS if dx]
    greeted += [device(d, 0) for d in range(-RADIUS, RADIUS + 1) if d]
    greeted += plane
    for dev in greeted:
        pl.semaphore_signal(barrier, inc=1, device_id=dev, device_id_type=MESH)

    keep_s = jnp.where(by == 0, F32(0.0), F32(1.0))
    keep_n = jnp.where(by == nby - 1, F32(0.0), F32(1.0))
    lane8 = lanes_of((8, COLS))
    sub8 = lax.broadcasted_iota(jnp.int32, (8, COLS), 0)

    loads[0].wait()
    depth_v[...] = kmt_v[...].astype(F32)
    for f in range(3):
        loads[1 + f].wait()
        pad = pads[f]

        quads = []
        for c in range(KL // CHUNK):
            packed = jnp.zeros((8, COLS), F32)
            for l in range(CHUNK):
                k = c * CHUNK + l
                tile = raw[f, k]
                pad[PITCH * (k + 1) : PITCH * (k + 1) + 8, :] = tile
                packed = jnp.where(lane8 // 4 == k % 32, roll(tile, 2 + 4 * (k % 32), 1), packed)
            quads.append(packed)
        tx_col[2 * f] = (quads[0] + quads[1]) + (quads[2] + quads[3])
        tx_col[2 * f + 1] = quads[4] + quads[5]
    tx_col[6] = depth_v[...]

    def edge_row(f, row):
        return pads[f][pl.ds(PITCH + row, KL, stride=PITCH), :]

    lane_row = lanes_of((8, COLS))
    for side, (row, inner) in enumerate([(0, 1), (ROWS - 1, ROWS - 2)]):
        edges = [edge_row(f, row) for f in range(3)]
        tx_row1[side, 0:KL] = edges[0]
        tx_row1[side, KL : 2 * KL] = edge_row(0, inner)
        tx_row1[side, 2 * KL : 3 * KL] = edges[1]
        tx_row1[side, 3 * KL : 4 * KL] = edges[2]
        tx_row1[side, 4 * KL : 4 * KL + 8] = depth_v[...]
        tx_row2[side, 0:KL] = edge_row(1, inner)
        tx_row2[side, KL : 2 * KL] = edge_row(2, inner)
        corner = jnp.zeros((8, COLS), F32)
        for f in range(3):
            for g in range(6):
                at = 2 * (6 * f + g)
                corner = jnp.where(lane_row // 2 == at // 2, roll(edges[f][8 * g : 8 * g + 8], 1 + at, 1), corner)
        tx_cor[side, 0:8] = depth_v[...]
        tx_cor[side, 8:16] = corner
        for i in range(6):
            tx_cor[side, 16 + i : 17 + i] = tx_col[i, row : row + 1]
        tx_cor[side, 22:24] = jnp.zeros((2, COLS), F32)

    def remote(src, dst, send, recv, dev):
        return pltpu.make_async_remote_copy(
            src_ref=src, dst_ref=dst, send_sem=send, recv_sem=recv, device_id=dev, device_id_type=MESH
        )

    pl.semaphore_wait(barrier, len(greeted))

    south, north, west, east = device(-1, 0), device(1, 0), device(0, -1), device(0, 1)
    row1 = [
        remote(tx_row1.at[0], rx_row1.at[1], row1_s.at[0], row1_r.at[1], south),
        remote(tx_row1.at[1], rx_row1.at[0], row1_s.at[1], row1_r.at[0], north),
    ]
    cols = [
        remote(tx_col, rx_col.at[1], col_s.at[0], col_r.at[1], west),
        remote(tx_col, rx_col.at[0], col_s.at[1], col_r.at[0], east),
    ]
    diagonal = [SW, SE, NW, NE]
    cors = []
    for i, d in enumerate(diagonal):
        dy, dx = DIRS[d]
        cors.append(
            remote(tx_cor.at[0 if dy < 0 else 1], rx_cor.at[3 - i], cor_s.at[i], cor_r.at[3 - i], device(dy, dx))
        )
    row2 = [
        remote(tx_row2.at[0], rx_row2.at[1], row2_s.at[0], row2_r.at[1], south),
        remote(tx_row2.at[1], rx_row2.at[0], row2_s.at[1], row2_r.at[0], north),
    ]
    first = row1 + cols + cors
    for copy in first + row2:
        copy.start()

    def tell(step):
        for d in (-(RADIUS << step), RADIUS << step):
            pl.semaphore_signal(known.at[step], inc=1, device_id=device(d, 0), device_id_type=MESH)
        for dev in plane:
            pl.semaphore_signal(known.at[3 + step], inc=1, device_id=dev, device_id_type=MESH)

    def told_by(step):
        pl.semaphore_wait(known.at[step], 2)

    def told_bx(step):
        pl.semaphore_wait(known.at[3 + step], len(plane))

    tell(0)

    for star in stars:
        star[0:PITCH, :] = jnp.zeros((PITCH, COLS), F32)
        star[PADDED - PITCH : PADDED, :] = jnp.zeros((PITCH, COLS), F32)

    def chunk_rows(ref, c):
        return ref.at[pl.ds(pl.multiple_of(c * (PITCH * CHUNK), PITCH * CHUNK), PITCH * (CHUNK + 2)), :]

    inside = [
        depth_v[...],
        jnp.where(lane8 == COLS - 1, F32(0.0), roll(depth_v[...], -1, 1)),
        jnp.where(lane8 == 0, F32(0.0), roll(depth_v[...], 1, 1)),
        jnp.where(sub8 == ROWS - 1, F32(0.0), roll(depth_v[...], -1, 0)),
        jnp.where(sub8 == 0, F32(0.0), roll(depth_v[...], 1, 0)),
    ]

    def star_inside(c, carry):
        views = [chunk_rows(pad, c) for pad in pads]
        out = chunk_rows(star_t, c)
        for l in range(CHUNK):
            base = PITCH * (l + 1)
            level = (c * CHUNK + l).astype(F32)
            terms = star_terms(level, inside, views[1][pl.ds(base, 8), :], views[2][pl.ds(base, 8), :])
            cell = views[0][pl.ds(base, 8), :]
            e = jnp.where(lane8 == COLS - 1, F32(0.0), roll(cell, -1, 1))
            w = jnp.where(lane8 == 0, F32(0.0), roll(cell, 1, 1))
            n = jnp.where(sub8 == ROWS - 1, F32(0.0), roll(cell, -1, 0))
            s = jnp.where(sub8 == 0, F32(0.0), roll(cell, 1, 0))
            out[pl.ds(base, 8), :] = star_value(terms, cell, (e, w, n, s))
            smooth = [jnp.where(level < d, F32(STEP_SMOOTH), F32(0.0)) for d in inside[1:]]
            up = jnp.where(level + F32(1.0) < inside[0], F32(STEP_VERT), F32(0.0))
            down = jnp.where(level > F32(0.0), F32(STEP_VERT), F32(0.0))
            own_ref[c * CHUNK + l] = F32(1.0) - (((smooth[0] + smooth[1]) + (smooth[2] + smooth[3])) + (up + down))
        return carry

    lax.fori_loop(0, KL // CHUNK, star_inside, 0)

    told_by(0)
    told_bx(0)
    tell(1)
    for copy in first:
        copy.wait_recv()

    dep = {
        S: keep_s * rx_row1[0, 4 * KL : 4 * KL + 8],
        N: keep_n * rx_row1[1, 4 * KL : 4 * KL + 8],
        W: rx_col[0, 6],
        E: rx_col[1, 6],
        SW: keep_s * rx_cor[0, 0:8],
        SE: keep_s * rx_cor[1, 0:8],
        NW: keep_n * rx_cor[2, 0:8],
        NE: keep_n * rx_cor[3, 0:8],
    }

    def patch(own, near):
        beside = jnp.where(lane8 < 64, near[E], near[W])
        below = jnp.where(sub8 < 4, near[N], near[S])
        across = jnp.where(
            sub8 < 4, jnp.where(lane8 < 64, near[NE], near[NW]), jnp.where(lane8 < 64, near[SE], near[SW])
        )
        return jnp.concatenate(
            [jnp.concatenate([own, beside], axis=1), jnp.concatenate([below, across], axis=1)], axis=0
        )

    depth = patch(depth_v[...], dep)
    depths = (depth, roll(depth, -1, 1), roll(depth, 1, 1), roll(depth, -1, 0), roll(depth, 1, 0))
    for i, d in enumerate(depths):
        depths_v[i] = d

    rows1 = {}
    for side, (keep, place) in enumerate([(keep_s, PITCH - 1), (keep_n, PITCH + ROWS)]):
        for f, at in ((0, 0), (1, 2), (2, 3)):
            value = keep * rx_row1[side, at * KL : (at + 1) * KL]
            pads[f][pl.ds(place, KL, stride=PITCH), :] = value
            rows1[side, f] = value

    odd = lane8 % 4 >= 2
    for i in range(6):
        q_ref[i] = jnp.where(odd, rx_col[1, i], rx_col[0, i])
    lane_corner = [
        keep * jnp.where(odd, rx_cor[2 * side + 1, 16:24], rx_cor[2 * side, 16:24])
        for side, keep in enumerate((keep_s, keep_n))
    ]
    level_corner = [
        keep * jnp.where(lane8 % 2 == 1, rx_cor[2 * side + 1, 8:16], rx_cor[2 * side, 8:16])
        for side, keep in enumerate((keep_s, keep_n))
    ]

    level_rows = lax.broadcasted_iota(jnp.int32, (KL, COLS), 0).astype(F32)

    def star_rows(fields, second):
        for side, (row, place) in enumerate([(2 * ROWS - 1, PITCH - 1), (ROWS, PITCH + ROWS)]):
            near = [depths_v[i, row : row + 1, 0:COLS] for i in range(5)]
            terms = star_terms(level_rows, near, rows1[side, 1], rows1[side, 2])
            for f in fields:
                cell = rows1[side, f]
                inner = edge_row(f, 0 if side == 0 else ROWS - 1)
                outer = second(side, f)
                edge = jnp.concatenate(
                    [roll(level_corner[side], COLS - 1 - 2 * (6 * f + g), 1) for g in range(6)], axis=0
                )
                e, w = east_west(cell, edge)
                n, s = (inner, outer) if side == 0 else (outer, inner)
                stars[f][pl.ds(place, KL, stride=PITCH), :] = star_value(terms, cell, (e, w, n, s))

    def star_cols(fields):
        near = [
            jnp.where(odd, depths_v[i, 0:8, COLS : COLS + 1], depths_v[i, 0:8, 2 * COLS - 1 : 2 * COLS]) for i in range(5)
        ]
        for half in range(2):
            level = (lane8 // 4 + 32 * half).astype(F32)
            terms = star_terms(level, near, q_ref[2 + half], q_ref[4 + half])
            for f in fields:
                i = 2 * f + half
                cell, own = q_ref[i], tx_col[i]
                e = jnp.where(odd, roll(cell, -1, 1), roll(own, -1, 1))
                w = jnp.where(odd, roll(own, 1, 1), roll(cell, 1, 1))
                n = jnp.where(sub8 == ROWS - 1, lane_corner[1][i : i + 1], roll(cell, -1, 0))
                s = jnp.where(sub8 == 0, lane_corner[0][i : i + 1], roll(cell, 1, 0))
                qs_ref[i] = star_value(terms, cell, (e, w, n, s))

    def near_own():
        return [depths_v[i, 0:8, 0:COLS] for i in range(5)]

    def edge_of(ref, f, c, l):
        shift = lax.rem(2 * COLS - 2 - 32 * lax.rem(c, 4) - 4 * l, COLS)
        return roll(ref[2 * f + c // 4], shift, 1)

    def star_own(fields, unroll):
        def step(c, carry):
            near = near_own()
            views = [chunk_rows(pad, c) for pad in pads]
            outs = [chunk_rows(star, c) for star in stars]
            for l in range(CHUNK):
                base = PITCH * (l + 1)
                level = (c * CHUNK + l).astype(F32)
                terms = star_terms(
                    level, near, views[1][pl.ds(base, 8), :], views[2][pl.ds(base, 8), :]
                )
                for f in fields:
                    cell = views[f][pl.ds(base, 8), :]
                    e, w = east_west(cell, edge_of(q_ref, f, c, l))
                    n = views[f][pl.ds(base + 1, 8), :]
                    s = views[f][pl.ds(base - 1, 8), :]
                    outs[f][pl.ds(base, 8), :] = star_value(terms, cell, (e, w, n, s))
            return carry

        lax.fori_loop(0, KL // CHUNK, step, 0, unroll=unroll)

    def update_own(fields, unroll):
        def step(c, total):
            near = near_own()
            views = [chunk_rows(star, c) for star in stars]
            for l in range(CHUNK):
                base = PITCH * (l + 1)
                level = (c * CHUNK + l).astype(F32)
                smooth = [jnp.where(level < d, F32(STEP_SMOOTH), F32(0.0)) for d in near[1:]]
                up = jnp.where(level + F32(1.0) < near[0], F32(STEP_VERT), F32(0.0))
                down = jnp.where(level > F32(0.0), F32(STEP_VERT), F32(0.0))
                own = F32(1.0) - (((smooth[0] + smooth[1]) + (smooth[2] + smooth[3])) + (up + down))
                centre = level < near[0]
                for f in fields:
                    view = views[f]
                    cell = view[pl.ds(base, 8), :]
                    e, w = east_west(cell, edge_of(qs_ref, f, c, l))
                    n = view[pl.ds(base + 1, 8), :]
                    s = view[pl.ds(base - 1, 8), :]
                    above = view[pl.ds(base + PITCH, 8), :]
                    below = view[pl.ds(base - PITCH, 8), :]
                    value = own * cell + F32(STEP_SMOOTH) * ((e + w) + (n + s)) + F32(STEP_VERT) * (above + below)
                    value = jnp.where(centre, value, F32(0.0))
                    fresh[f][c * CHUNK + l] = value
                    if f == 0:
                        total = total + value
            return total

        return lax.fori_loop(0, KL // CHUNK, step, jnp.zeros((8, COLS), F32), unroll=unroll)

    def add_beyond():
        for side, row in enumerate((0, ROWS - 1)):
            cell, halo = edge_row(0, row), rows1[side, 0]
            adv = F32(0.5 * STEP_ADV) * edge_row(2, row)
            centre = level_rows < depths_v[0, row : row + 1, 0:COLS]
            beyond = level_rows < depths_v[4 - side, row : row + 1, 0:COLS]
            more = jnp.where(beyond, F32(STEP_DIFF) * (halo - cell), F32(0.0))
            more = more + adv * halo if side == 0 else more - adv * halo
            place = pl.ds(PITCH + row, KL, stride=PITCH)
            star_t[place, :] = star_t[place, :] + jnp.where(centre, more, F32(0.0))
        here = jnp.where(odd, depth_v[:, 0:1], depth_v[:, COLS - 1 : COLS])
        near = jnp.where(odd, depths_v[0, 0:8, 2 * COLS - 1 : 2 * COLS], depths_v[0, 0:8, COLS : COLS + 1])
        for half in range(2):
            level = (lane8 // 4 + 32 * half).astype(F32)
            cell = tx_col[half]
            halo = jnp.where(odd, roll(q_ref[half], 1, 1), roll(q_ref[half], -1, 1))
            adv = F32(0.5 * STEP_ADV) * tx_col[2 + half] * halo
            more = jnp.where(level < near, F32(STEP_DIFF) * (halo - cell), F32(0.0)) + jnp.where(odd, adv, -adv)
            beyond_ref[half] = jnp.where(level < here, more, F32(0.0))
        rim = jnp.logical_or(lane8 == 0, lane8 == COLS - 1)
        for k in range(KL):
            place = pl.ds(PITCH * (k + 1), 8)
            edge = roll(beyond_ref[k // 32], COLS - 2 - 4 * (k % 32), 1)
            star_t[place, :] = star_t[place, :] + jnp.where(rim, edge, F32(0.0))

    def update_tracer():
        rim_rows = jnp.where(sub8 == 0, depths_v[4, 0:8, 0:COLS], F32(0.0))
        rim_rows = jnp.where(sub8 == ROWS - 1, depths_v[3, 0:8, 0:COLS], rim_rows)
        rim_lanes = jnp.where(lane8 == 0, depths_v[2, 0:8, 0:COLS], F32(0.0))
        rim_lanes = jnp.where(lane8 == COLS - 1, depths_v[1, 0:8, 0:COLS], rim_lanes)
        depth_own = depth_v[...]
        total = [jnp.zeros((8, COLS), F32)] * 4
        for k in range(KL):
            base = PITCH * (k + 1)
            cell = star_t[pl.ds(base, 8), :]
            e, w = east_west(cell, roll(qs_ref[k // 32], COLS - 2 - 4 * (k % 32), 1))
            n = star_t[pl.ds(base + 1, 8), :]
            s = star_t[pl.ds(base - 1, 8), :]
            above = star_t[pl.ds(base + PITCH, 8), :]
            below = star_t[pl.ds(base - PITCH, 8), :]
            own = own_ref[k] - jnp.where(rim_rows > F32(k), F32(STEP_SMOOTH), F32(0.0))
            own = own - jnp.where(rim_lanes > F32(k), F32(STEP_SMOOTH), F32(0.0))
            value = own * cell + F32(STEP_SMOOTH) * ((e + w) + (n + s)) + F32(STEP_VERT) * (above + below)
            value = jnp.where(depth_own > F32(k), value, F32(0.0))
            temp_out[k] = value
            total[k % 4] = total[k % 4] + value
        return (total[0] + total[1]) + (total[2] + total[3])

    add_beyond()
    star_rows([0], lambda side, f: (keep_s, keep_n)[side] * rx_row1[side, KL : 2 * KL])
    star_cols([0])
    rhs = update_tracer() * F32(1.0 / math.sqrt(KL))

    height = depths_v[0] * F32(1.0 / KL)
    w_e = jnp.minimum(height, roll(height, -1, 1))
    w_n = jnp.minimum(height, roll(height, -1, 0))
    w_w = roll(w_e, 1, 1)
    w_s = roll(w_n, 1, 0)
    diag = F32(SURFACE_TERM) + w_e + w_w + w_n + w_s
    inverse = F32(1.0) / diag
    scaled = (w_e * inverse, w_w * inverse, w_n * inverse, w_s * inverse)

    tx_u[...] = rhs * inverse[0:8, 0:COLS]
    round_u = [
        remote(tx_u, rx_u.at[7 - i], u_s.at[i], u_r.at[7 - i], device(dy, dx)) for i, (dy, dx) in enumerate(DIRS)
    ]
    for copy in round_u:
        copy.start()
    told_by(1)
    told_bx(1)
    tell(2)
    for copy in round_u:
        copy.wait_recv()

    power = patch(tx_u[...], {d: rx_u[d] for d in range(8)})
    largest = jnp.max(jnp.max(jnp.abs(power), axis=0, keepdims=True), axis=1, keepdims=True)
    powers = [power]
    for _ in range(ITERS):
        e, w = roll(power, -1, 1), roll(power, 1, 1)
        n, s = roll(power, -1, 0), roll(power, 1, 0)
        power = (scaled[0] * e + scaled[1] * w) + (scaled[2] * n + scaled[3] * s)
        powers.append(power)
    own_diag = diag[0:8, 0:COLS]
    powers = [p[0:8, 0:COLS] for p in powers]
    steps = [powers[i] - powers[i + 1] for i in range(ITERS)]

    count = len(GRAM)
    grid = F32(4096.0 * 4.5) * largest * largest
    finer = grid * F32(1.0 / 4096.0)
    levels = ([], [], [])
    for i, j in GRAM:
        head, tail = two_prod(powers[i], powers[j])
        wide, extra = two_prod(own_diag, head)
        extra = extra + own_diag * tail
        coarse = (wide + grid) - grid
        wide = wide - coarse
        fine = (wide + finer) - finer
        for held, part in zip(levels, (coarse, fine, (wide - fine) + extra)):
            held.append(part)
    tiles = levels[0] + levels[1] + levels[2]
    tiles += [jnp.zeros((8, COLS), F32)] * (-len(tiles) % 8)
    row = jnp.zeros((8, COLS), F32)
    for c, tile in enumerate(sum_rows(tiles)):
        row = row + jnp.where(lane8 == sub8 + 8 * c, jnp.sum(tile, axis=1, keepdims=True), F32(0.0))
    row = jnp.sum(row, axis=0, keepdims=True)
    lane1 = lanes_of((1, COLS))
    last = jnp.logical_and(lane1 >= 2 * count, lane1 < 3 * count)

    tx_bx[...] = row
    told_bx(2)
    over_bx = [
        remote(tx_bx, rx_bx.at[o - 1], bx_s, bx_r, device(0, o)) for o in range(1, nbx)
    ]
    for copy in over_bx:
        copy.start()
    remote(rx_bx, rx_bx, bx_s, bx_r, east).wait_recv()
    row, lost = add_exact([row] + [rx_bx[i] for i in range(nbx - 1)])
    row = row + jnp.where(last, roll(lost, 2 * count, 1) + roll(lost, count, 1), F32(0.0))

    told_by(2)
    tx_by[...] = row
    rx_by[0:1, :] = row
    order = sorted(range(1, nby), key=lambda o: -min(o, nby - o))
    over_by = [remote(tx_by, rx_by.at[pl.ds(o, 1), :], by_s, by_r, device(o, 0)) for o in order]
    for copy in over_by:
        copy.start()

    for copy in row2:
        copy.wait_recv()
    star_rows([1, 2], lambda side, f: (keep_s, keep_n)[side] * rx_row2[side, (f - 1) * KL : f * KL])
    star_cols([1, 2])
    star_own([1, 2], 1)
    update_own([1, 2], 1)
    for copy in first + row2 + round_u:
        copy.wait_send()
    remote(rx_bx, rx_bx, bx_s, bx_r, east).wait_send()

    others = rx_by.at[pl.ds(1, nby - 1), :]
    remote(others, others, by_s, by_r, north).wait_recv()
    row, lost = add_exact([rx_by[i : i + 8] for i in range(0, nby, 8)])
    for shift in (4, 2, 1):
        row, more = two_sum(row, roll(row, shift, 0))
        lost = (lost + roll(lost, shift, 0)) + more
    row, lost = row[0:1], lost[0:1]
    head, tail = two_sum(row, roll(row, -count, 1))
    total = quick_sum(head, tail + ((roll(row, -2 * count, 1) + lost) + roll(lost, -count, 1)))

    gram = {}
    for k, (i, j) in enumerate(GRAM):
        gram[i, j] = gram[j, i] = tuple(jnp.broadcast_to(part[0:1, k : k + 1], (8, COLS)) for part in total)
    system = [[sub2(gram[i, j], gram[i, j + 1]) for j in range(ITERS)] + [gram[i, 0]] for i in range(ITERS)]
    top = system[0]
    over = F32(1.0) / top[0][0]
    lower = []
    for i in (1, 2):
        ratio = system[i][0][0] * over
        left = []
        for j in range(ITERS + 1):
            head, tail = two_prod(ratio, top[j][0])
            value, lost = two_sum(system[i][j][0], -head)
            left.append((value, lost + (system[i][j][1] - (tail + ratio * top[j][1]))))
        ratio = (left[0][0] + left[0][1]) * over
        lower.append([quick_sum(left[j][0], left[j][1] - ratio * top[j][0]) for j in range(1, ITERS + 1)])
    (a11, a12, b1), (a21, a22, b2) = lower
    det = F32(1.0) / minor(a11, a22, a12, a21)
    c1 = minor(b1, a22, b2, a12) * det
    c2 = minor(b2, a11, b1, a21) * det
    c0 = ((top[3][0] - top[1][0] * c1) - top[2][0] * c2) * over

    surface = (c0 * powers[0] + c1 * powers[1]) + c2 * powers[2]
    resid = own_diag * (((powers[0] - c0 * steps[0]) - c1 * steps[1]) - c2 * steps[2])
    surface_out[...] = surface
    resid_out[...] = resid
    remote(others, others, by_s, by_r, north).wait_send()


def store(*refs):
    sources, targets, sems = refs[:5], refs[5:10], refs[10]
    copies = [pltpu.make_async_copy(src, dst, sems.at[i]) for i, (src, dst) in enumerate(zip(sources, targets))]
    for copy in copies:
        copy.start()
    for copy in copies:
        copy.wait()


def solution(mesh):
    nby, nbx = mesh.shape["by"], mesh.shape["bx"]

    def on_device(temp, uvel, vvel, kmt):
        field = jax.ShapeDtypeStruct(temp.shape, F32)
        plane = jax.ShapeDtypeStruct(kmt.shape, F32)
        vmem, dma = pltpu.VMEM, pltpu.SemaphoreType.DMA
        results = pl.pallas_call(
            lambda *refs: kernel(nby, nbx, *refs),
            out_shape=(*[pltpu.VMEM(temp.shape, F32)] * 3, *[pltpu.VMEM(kmt.shape, F32)] * 2),
            in_specs=[pl.BlockSpec(memory_space=pltpu.HBM)] * 4,
            out_specs=(pl.BlockSpec(memory_space=pltpu.VMEM),) * 5,
            scratch_shapes=[
                vmem((3, KL, ROWS, COLS), F32),
                vmem((ROWS, COLS), jnp.int32),
                *[vmem((PADDED, COLS), F32)] * 6,
                vmem((ROWS, COLS), F32),
                vmem((5, 2 * ROWS, 2 * COLS), F32),
                vmem((6, ROWS, COLS), F32),
                vmem((6, ROWS, COLS), F32),
                vmem((KL, ROWS, COLS), F32),
                vmem((2, ROWS, COLS), F32),
                vmem((2, 4 * KL + 8, COLS), F32),
                vmem((2, 2 * KL, COLS), F32),
                vmem((7, ROWS, COLS), F32),
                vmem((2, 24, COLS), F32),
                vmem((2, 4 * KL + 8, COLS), F32),
                vmem((2, 2 * KL, COLS), F32),
                vmem((2, 7, ROWS, COLS), F32),
                vmem((4, 24, COLS), F32),
                vmem((ROWS, COLS), F32),
                vmem((8, ROWS, COLS), F32),
                vmem((1, COLS), F32),
                vmem((nbx - 1, 1, COLS), F32),
                vmem((1, COLS), F32),
                vmem((nby, COLS), F32),
                dma((4,)),
                dma((2,)), dma((2,)), dma((2,)), dma((2,)),
                dma((2,)), dma((2,)), dma((4,)), dma((4,)),
                dma((8,)), dma((8,)),
                dma, dma, dma, dma,
                pltpu.SemaphoreType.REGULAR((6,)),
            ],
            compiler_params=pltpu.CompilerParams(
                collective_id=0, has_side_effects=True, vmem_limit_bytes=32 * 1024 * 1024
            ),
        )(*[pltpu.with_memory_space_constraint(a, pltpu.HBM) for a in (temp, uvel, vvel, kmt)])
        return pl.pallas_call(
            store,
            out_shape=(field, field, field, plane, plane),
            in_specs=[pl.BlockSpec(memory_space=pltpu.VMEM)] * 5,
            out_specs=(pl.BlockSpec(memory_space=pltpu.HBM),) * 5,
            scratch_shapes=[dma((5,))],
            name="store",
        )(*[pltpu.with_memory_space_constraint(r, pltpu.VMEM) for r in results])

    in_specs = (P(None, "by", "bx"), P(None, "by", "bx"), P(None, "by", "bx"), P("by", "bx"))
    out_specs = (
        P(None, "by", "bx"),
        P(None, "by", "bx"),
        P(None, "by", "bx"),
        P("by", "bx"),
        P("by", "bx"),
    )
    return jax.shard_map(on_device, mesh=mesh, in_specs=in_specs, out_specs=out_specs, check_vma=False)
```
